256 devices in a mesh: particle: 32 (over z, x_lo, core), space: 8 (over x_hi, y).
Axes of the slice: x: 4 (x_hi: 2, x_lo: 2; x = x_hi * 2 + x_lo), y: 4, z: 8, core: 2. Of those that a mesh axis runs over, the one named last changes fastest.
Arguments:
- coeffs: float32 [32, 4096], P('particle'), may hold values from -1.6 to 1.6
- modes: int32 [4096], replicated, may hold values from 0 to 4095, each once
- basis_x: float32 [128, 16], replicated, may hold values from -1.5 to 1.5
- basis_y: float32 [128, 16], replicated, may hold values from -1.5 to 1.5
- basis_z: float32 [128, 16], replicated, may hold values from -1.5 to 1.5
- pressure: float32 [32, 128, 128, 128], P('particle', 'space'), may hold values from -6 to 6
- initial_adjoint: float32 [32, 128, 128, 128], P('particle', 'space'), may hold values from -3 to 3
- sensors: int32 [1024], replicated, may hold values from 0 to 2097151, as said below
- observed: float32 [1024], replicated, may hold values from -6 to 6
- precision: float32 [1024], replicated, may hold values from 0.5 to 2
Outputs:
- new_coeffs: float32 [32, 4096], P('particle', 'space')
- adjoint: float32 [32, 128, 128, 128], P('particle', 'space')
The draws below stay inside these ranges and needn't reach their ends.
Inputs may be any that keep to these rules, and one draw needn't show every extreme that they name: The sensors are distinct and increasing; sensor s lies in the run of 2048 consecutive flat cells starting at s times that run.
All inputs are finite; a program needn't handle non-finite values.
Results may differ from the reference program's by a relative error of at most 0.0017.
Values sent between devices are 32-bit elements; how exact they have to be, the bound alone decides.
A program may use at most 64 MiB of HBM per device.

```python
import math
import jax
import jax.numpy as jnp
from jax import lax

M = 16
K = 4096
NY = 128
NZ = 128
S = 1024
ITERS = 2
NX = 128
PARTICLES = 32


def draw_coeffs(key, part):
    key_center = jax.random.fold_in(key, 11)
    key_spread = jax.random.fold_in(key, 12)
    key_offset = jax.random.fold_in(key, 13)
    key_scale = jax.random.fold_in(key, 14)
    center = jax.random.uniform(key_center, (K,), jnp.float32, -1.5, 1.5)
    spread = 0.0003 * jnp.exp(jax.random.uniform(key_spread, (K,), jnp.float32) * jnp.log(4.0))
    member = jnp.exp(jax.random.uniform(key_scale, (PARTICLES,), jnp.float32, -1.0, 1.0) * jnp.log(4.0))
    offset = jax.random.truncated_normal(key_offset, -3.0, 3.0, (PARTICLES, K), jnp.float32)
    return (center[None, :] + member[:, None] * spread[None, :] * offset).astype(jnp.float32)


def draw_sensors(key, part):
    run_cells = NX * NY * NZ // S
    offsets = jax.random.randint(jax.random.fold_in(key, 21), (S,), 0, run_cells)
    return (jnp.arange(S, dtype=jnp.int32) * run_cells + offsets).astype(jnp.int32)


def block_scale(own_key, shape, shards, smallest, high):
    def one(position, blocks):
        draws = jax.random.uniform(jax.random.fold_in(jax.random.fold_in(own_key, 6), position), (blocks,), jnp.float32, smallest / len(shards), high / len(shards))
        return jnp.repeat(jnp.exp(draws), shape[position] // blocks).reshape((-1,) + (1,) * (len(shape) - position - 1))

    gain = one(*shards[0])
    for cut in shards[1:]:
        gain = gain * one(*cut)
    return gain


def bell_draw(own_key, shape, scale, reach, cuts=(), kind=jnp.bfloat16):
    array = jax.random.normal(own_key, shape, jnp.float32) * scale
    if len(cuts) > 0:
        array = block_scale(own_key, shape, cuts, -0.22, 0.18) * array
    return jnp.clip(array, min=-reach, max=reach).astype(kind)


def setup_inputs(seed: int = 0) -> dict:
    arg_keys = jax.random.split(jax.random.key(seed), 11)
    coeffs = draw_coeffs(jax.random.fold_in(arg_keys[10], 71), 0)
    modes = jax.random.permutation(arg_keys[1], K).astype(jnp.int32)
    basis_x = bell_draw(arg_keys[2], (NX, M), M ** -0.5, 1.5, (), jnp.float32)
    basis_y = bell_draw(arg_keys[3], (NY, M), M ** -0.5, 1.5, (), jnp.float32)
    basis_z = bell_draw(arg_keys[4], (NZ, M), M ** -0.5, 1.5, (), jnp.float32)
    pressure = bell_draw(arg_keys[5], (PARTICLES, NX, NY, NZ), 1.0, 6.0, ((0, 32), (1, 8)), jnp.float32)
    initial_adjoint = bell_draw(arg_keys[6], (PARTICLES, NX, NY, NZ), 0.5, 3.0, ((0, 32), (1, 8)), jnp.float32)
    sensors = draw_sensors(jax.random.fold_in(arg_keys[10], 71), 0)
    observed = bell_draw(arg_keys[8], (S,), 1.0, 6.0, (), jnp.float32)
    precision = jnp.clip(jnp.exp(jax.random.uniform(arg_keys[9], (S,), jnp.float32, math.log(0.5), math.log(2.0))), 0.5, 2.0)
    return dict(coeffs=coeffs, modes=modes, basis_x=basis_x, basis_y=basis_y, basis_z=basis_z, pressure=pressure, initial_adjoint=initial_adjoint, sensors=sensors, observed=observed, precision=precision)


HIGH = lax.Precision.HIGHEST
STEP = 0.5
MID = slice(1, -1)
SHIFTS = ((slice(2, None), MID, MID), (slice(None, -2), MID, MID), (MID, slice(2, None), MID), (MID, slice(None, -2), MID), (MID, MID, slice(2, None)), (MID, MID, slice(None, -2)))


def log_field(xi, modes, x_rows, basis_y, basis_z):
    flat = jnp.zeros((M * M * M,), jnp.float32).at[modes].set(xi)
    tensor = flat.reshape(M, M, M)
    first = jnp.einsum("ijl,zl->ijz", tensor, basis_z, precision=HIGH)
    second = jnp.einsum("ijz,yj->iyz", first, basis_y, precision=HIGH)
    return jnp.einsum("iyz,xi->xyz", second, x_rows, precision=HIGH)


def apply_op(v_pad, kap_pad):
    center = v_pad[MID, MID, MID]
    kap_mid = kap_pad[MID, MID, MID]
    total = jnp.zeros_like(center)
    for shift in SHIFTS:
        total = total + 0.5 * (kap_mid + kap_pad[shift]) * (center - v_pad[shift])
    return total


def project(cellgrad, x_rows, basis_y, basis_z):
    first = jnp.einsum("xyz,zl->xyl", cellgrad, basis_z, precision=HIGH)
    second = jnp.einsum("xyl,yj->xjl", first, basis_y, precision=HIGH)
    return jnp.einsum("xjl,xi->ijl", second, x_rows, precision=HIGH).reshape(-1)


def reference(coeffs, modes, basis_x, basis_y, basis_z, pressure, initial_adjoint, sensors, observed, precision):
    index_x = jnp.arange(NX)[:, None, None]
    index_y = jnp.arange(NY)[None, :, None]
    index_z = jnp.arange(NZ)[None, None, :]
    edges = (index_x == NX - 1, index_x == 0, index_y == NY - 1, index_y == 0, index_z == NZ - 1, index_z == 0)
    factors = [0.5 + 0.5 * edge.astype(jnp.float32) for edge in edges]

    def one_particle(items):
        xi, field_p, warm_start = items
        kappa = jnp.exp(log_field(xi, modes, basis_x, basis_y, basis_z))
        kap_pad = jnp.pad(kappa, 1, mode="edge")
        picks = field_p.reshape(-1)[sensors]
        weighted = (picks - observed) * precision
        rhs = jnp.zeros((NX * NY * NZ,), jnp.float32).at[sensors].set(weighted).reshape(NX, NY, NZ)
        solved = warm_start
        resid = rhs - apply_op(jnp.pad(warm_start, 1), kap_pad)
        direction = resid
        norm_now = jnp.sum(resid * resid)
        for step in range(ITERS):
            image = apply_op(jnp.pad(direction, 1), kap_pad)
            alpha = norm_now / jnp.sum(direction * image)
            solved = solved + alpha * direction
            resid = resid - alpha * image
            if step + 1 < ITERS:
                norm_next = jnp.sum(resid * resid)
                direction = resid + (norm_next / norm_now) * direction
                norm_now = norm_next
        lam_pad = jnp.pad(solved, 1)
        pre_pad = jnp.pad(field_p, 1)
        total = jnp.zeros_like(rhs)
        for shift, factor in zip(SHIFTS, factors):
            total = total + factor * (solved - lam_pad[shift]) * (field_p - pre_pad[shift])
        cellgrad = kappa * total
        proj = project(cellgrad, basis_x, basis_y, basis_z)[modes]
        return -xi - proj, solved

    grads, adjoint = lax.map(one_particle, (coeffs, pressure, initial_adjoint))

    def distance_row(row):
        return jnp.sum((coeffs - row) ** 2, axis=1)

    dist = lax.map(distance_row, coeffs)
    width = jnp.sum(dist) / (PARTICLES * (PARTICLES - 1))
    kern = jnp.exp(-dist / width)

    def update_row(items):
        row, kern_col = items
        drive = jnp.sum(kern_col[:, None] * grads, axis=0)
        repel = jnp.sum(kern_col[:, None] * (row - coeffs), axis=0)
        return row + STEP * (drive + (2.0 / width) * repel) / PARTICLES

    new_coeffs = lax.map(update_row, (coeffs, kern.T))
    return new_coeffs, adjoint
```

```python
import jax
import jax.numpy as jnp
from jax import lax
from jax.experimental import pallas as pl
from jax.experimental.pallas import tpu as pltpu
from jax.sharding import PartitionSpec as P

F32 = jnp.float32
BF16 = jnp.bfloat16
NP = 32
NS = 8
LX = 16
NX = 128
NG = 128
M = 16
K = M * M * M
SH = K // NS
HALO = 3
STEP = 0.5
NN = (((1,), (1,)), ((), ()))


def pieces(value, count):
    out = []
    rest = value
    for _ in range(count):
        part = rest.astype(BF16)
        out.append(part)
        rest = rest - part.astype(F32)
    return out


def mm(a, b):
    return jnp.dot(a, b, preferred_element_type=F32)


def mm_nt(a, b):
    return lax.dot_general(a, b, NN, preferred_element_type=F32)


def fold(value):
    return jnp.sum(value.reshape(NG // 8, 8, NG), axis=0)


def kernel(
    c_hbm, modes_ref, bx_ref, by_ref, bz_ref, p_hbm, x_hbm, sens_ref, obs_ref, prec_ref,
    new_ref, adj_hbm,
    xe, pe, kp, kx, ky, kz, kb, u0, u1, xo, rsum, hot, lhot, lcs, bylhs, fbuf, pbuf, qbuf,
    cs, wk, pk, rp, gs, mom,
    in_sem, out_sem, halo_send, halo_recv, c_own, c_send, c_recv, m_send, m_recv, r_send, r_recv, g_send, g_recv,
):
    n = lax.axis_index("particle")
    s = lax.axis_index("space")
    first = s == 0
    last = s == NS - 1

    def peer_p(r):
        return {"particle": lax.rem(n + r, NP)}

    def peer_s(r):
        return {"space": lax.rem(s + r, NS)}

    barrier = pltpu.get_barrier_semaphore()

    def greet_s(r, carry):
        pl.semaphore_signal(barrier, inc=1, device_id=peer_s(r))
        return carry

    def greet_p(r, carry):
        pl.semaphore_signal(barrier, inc=1, device_id=peer_p(r))
        return carry

    lax.fori_loop(1, NS, greet_s, 0)
    lax.fori_loop(1, NP, greet_p, 0)

    load_x = pltpu.make_async_copy(x_hbm, xe.at[pl.ds(HALO, LX)], in_sem.at[0])
    load_p = pltpu.make_async_copy(p_hbm, pe.at[pl.ds(1, LX)], in_sem.at[1])
    load_c = pltpu.make_async_copy(c_hbm.at[s], cs.at[0], c_own)
    load_all = pltpu.make_async_copy(c_hbm, wk, in_sem.at[2])
    load_all.start()
    load_p.start()
    load_x.start()
    load_c.start()

    load_all.wait()
    row_id = lax.broadcasted_iota(jnp.int32, (M * M, NG), 0)
    sub_id = lax.broadcasted_iota(jnp.int32, (M, NG), 0)
    for chunk in range(K // NG):
        pos = modes_ref[chunk : chunk + 1, :]
        cols = slice(chunk * NG, (chunk + 1) * NG)
        upper = lax.shift_right_logical(pos, 4)
        lower = lax.bitwise_and(pos, 15)
        hot[:, cols] = jnp.where(row_id == upper, 1.0, 0.0).astype(BF16)
        low = jnp.where(sub_id == lower, 1.0, 0.0)
        lhot[:, cols] = low
        own = wk[chunk // 4, chunk % 4 : chunk % 4 + 1, :]
        for q, part in enumerate(pieces(own, 3)):
            lcs[q * M : (q + 1) * M, cols] = (low * part.astype(F32)).astype(BF16)

    pl.semaphore_wait(barrier, NS - 1 + NP - 1)

    up = {"space": jnp.minimum(s + 1, NS - 1)}
    down = {"space": jnp.maximum(s - 1, 0)}

    def remote(src, dst, send, recv, where):
        return pltpu.make_async_remote_copy(src_ref=src, dst_ref=dst, send_sem=send, recv_sem=recv, device_id=where)

    def x_up():
        return remote(x_hbm.at[pl.ds(LX - HALO, HALO)], xe.at[pl.ds(0, HALO)], halo_send.at[0], halo_recv.at[0], up)

    def x_down():
        return remote(x_hbm.at[pl.ds(0, HALO)], xe.at[pl.ds(HALO + LX, HALO)], halo_send.at[1], halo_recv.at[1], down)

    def p_up():
        return remote(p_hbm.at[pl.ds(LX - 1, 1)], pe.at[pl.ds(0, 1)], halo_send.at[2], halo_recv.at[2], up)

    def p_down():
        return remote(p_hbm.at[pl.ds(0, 1)], pe.at[pl.ds(LX + 1, 1)], halo_send.at[3], halo_recv.at[3], down)

    def r_up():
        return remote(rsum.at[pl.ds(LX, 2)], rsum.at[pl.ds(0, 2)], halo_send.at[4], halo_recv.at[4], up)

    def r_down():
        return remote(rsum.at[pl.ds(2, 2)], rsum.at[pl.ds(LX + 2, 2)], halo_send.at[5], halo_recv.at[5], down)

    @pl.when(jnp.logical_not(last))
    def _():
        x_up().start()

    @pl.when(jnp.logical_not(first))
    def _():
        x_down().start()

    @pl.when(jnp.logical_not(last))
    def _():
        p_up().start()

    @pl.when(jnp.logical_not(first))
    def _():
        p_down().start()

    def send_c(r, carry):
        remote(c_hbm.at[s], cs.at[NP - r], c_send, c_recv, peer_p(r)).start()
        return carry

    lax.fori_loop(1, NP, send_c, 0)

    @pl.when(first)
    def _():
        xe[0:HALO] = jnp.zeros((HALO, NG, NG), F32)
        pe[0:1] = jnp.zeros((1, NG, NG), F32)
        rsum[0:2] = jnp.zeros((2, 8, NG), F32)

    @pl.when(last)
    def _():
        xe[HALO + LX :] = jnp.zeros((HALO, NG, NG), F32)
        pe[LX + 1 :] = jnp.zeros((1, NG, NG), F32)
        rsum[LX + 2 :] = jnp.zeros((2, 8, NG), F32)

    flat = (
        lax.broadcasted_iota(jnp.int32, (M, NG), 0) * NG + lax.broadcasted_iota(jnp.int32, (M, NG), 1)
    )

    def sensor_of(layer, block):
        index = layer * 8 + block
        return index, sens_ref[index] - index * (M * NG)

    load_p.wait()

    def misfit(x, carry):
        for b in range(8):
            index, cell = sensor_of(s * LX + x, b)
            part = pe[x + 1, b * M : (b + 1) * M, :]
            hit = jnp.where(flat == cell, (part - obs_ref[index]) * prec_ref[index], 0.0)
            rsum[x + 2, b : b + 1, :] = jnp.sum(hit, axis=0, keepdims=True)
        return carry

    lax.fori_loop(0, LX, misfit, 0)

    @pl.when(jnp.logical_not(last))
    def _():
        r_up().start()

    @pl.when(jnp.logical_not(first))
    def _():
        r_down().start()

    eye = jnp.where(
        lax.broadcasted_iota(jnp.int32, (M, M), 0) == lax.broadcasted_iota(jnp.int32, (M, M), 1), 1.0, 0.0
    ).astype(BF16)
    by3 = pieces(by_ref[...], 3)
    bz3 = pieces(bz_ref[...], 3)
    bzt = [mm_nt(eye, part).astype(BF16) for part in bz3]
    byt = [mm_nt(eye, part).astype(BF16) for part in by3[:2]]
    for q, which in enumerate((0, 0, 1, 0, 1, 2)):
        bylhs[:, q * M : (q + 1) * M] = by3[which].astype(F32)
    lhs_y = bylhs[:, 0 : 6 * M].astype(BF16)

    xi = mm_nt(hot[...], lcs[...]).astype(BF16)
    field = mm(xi, jnp.concatenate([bzt[0]] * 3, axis=0))
    field = field + mm(xi, jnp.concatenate([bzt[1]] * 3, axis=0))
    field = field + mm(xi, jnp.concatenate([bzt[2]] * 3, axis=0))
    fbuf[...] = field.reshape(M, M, NG)

    lane = lax.broadcasted_iota(jnp.int32, (NG, NG), 1)
    suby = lax.broadcasted_iota(jnp.int32, (NG, NG), 0)
    inner_y = jnp.where(suby == NG - 1, 0.0, 0.5)
    inner_z = jnp.where(lane == NG - 1, 0.0, 0.5)
    rim = (
        jnp.where(suby == NG - 1, 1.0, 0.0)
        + jnp.where(suby == 0, 1.0, 0.0)
        + jnp.where(lane == NG - 1, 1.0, 0.0)
        + jnp.where(lane == 0, 1.0, 0.0)
    )

    def mix(e):
        g = jnp.clip(s * LX - HALO + e, 0, NX - 1)
        total = bx_ref[g, 0] * fbuf[0]
        for i in range(1, M):
            total = total + bx_ref[g, i] * fbuf[i]
        a, b, c = pieces(total, 3)
        return jnp.concatenate([a, b, a, c, b, a], axis=0)

    def faces(e, k, before):
        kp[e] = k
        ky[e] = inner_y * (k + pltpu.roll(k, NG - 1, 0))
        kz[e] = inner_z * (k + pltpu.roll(k, NG - 1, 1))
        kb[e] = rim * k
        kx[before] = 0.5 * (kp[before] + k)

    def log_layers(t, top):
        e = 2 * t
        both = jnp.exp(mm(lhs_y, jnp.concatenate([mix(e), mix(e + 1)], axis=1)))
        k0, k1 = both[:, :NG], both[:, NG:]
        faces(e, k0, jnp.maximum(e - 1, 0))
        faces(e + 1, k1, e)
        return jnp.maximum(top, jnp.max(jnp.maximum(k0, k1).reshape(NG // 8, 8, NG), axis=0))

    top = lax.fori_loop(0, HALO + LX // 2, log_layers, jnp.zeros((8, NG), F32))
    tau = (1.0 / 16.0) / jnp.max(top, keepdims=True)

    def apply(v_ref, i, e):
        v = v_ref[i]
        total = kb[e] * v
        total = total - kx[e] * (v_ref[i + 1] - v)
        total = total + kx[e - 1] * (v - v_ref[i - 1])
        fy = ky[e] * (pltpu.roll(v, NG - 1, 0) - v)
        total = total - (fy - pltpu.roll(fy, 1, 0))
        fz = kz[e] * (pltpu.roll(v, NG - 1, 1) - v)
        total = total - (fz - pltpu.roll(fz, 1, 1))
        return v, total

    def inside(g):
        return jnp.where(jnp.logical_and(g >= 0, g < NX), 1, 0)

    def put_u0(e):
        g = s * LX - 2 + e
        safe = jnp.clip(g, 0, NX - 1)
        _, image = apply(xe, e + 1, e + 1)
        load = []
        for b in range(8):
            _, cell = sensor_of(safe, b)
            load.append(jnp.where(flat == cell, rsum[e, b : b + 1, :], 0.0))
        value = jnp.concatenate(load, axis=0) - image
        u0[e] = jnp.where(inside(g) == 1, value, 0.0)

    def put_u1(e):
        g = s * LX - 1 + e
        _, image = apply(u0, e + 1, e + 2)
        u1[e] = jnp.where(inside(g) == 1, image * tau, 0.0)

    def moments(x, sums):
        second, image = apply(u1, x + 1, x + 3)
        start = u0[x + 2]
        m0, m1, m2, m3 = sums
        return (
            m0 + fold(start * start),
            m1 + fold(start * second),
            m2 + fold(second * second),
            m3 + fold(second * image),
        )

    def outer(t, count, width):
        return t + jnp.where(t >= width, count - 2 * width, 0)

    load_x.wait()
    lax.fori_loop(3, 17, lambda e, c: (put_u0(e), c)[1], 0)
    lax.fori_loop(3, 15, lambda e, c: (put_u1(e), c)[1], 0)
    zero = jnp.zeros((8, NG), F32)
    sums = lax.fori_loop(3, 13, moments, (zero, zero, zero, zero))

    @pl.when(jnp.logical_not(first))
    def _():
        x_up().wait_recv()
        r_up().wait_recv()

    @pl.when(jnp.logical_not(last))
    def _():
        x_down().wait_recv()
        r_down().wait_recv()

    lax.fori_loop(0, 6, lambda t, c: (put_u0(outer(t, LX + 4, 3)), c)[1], 0)
    lax.fori_loop(0, 6, lambda t, c: (put_u1(outer(t, LX + 2, 3)), c)[1], 0)
    sums = lax.fori_loop(0, 6, lambda t, c: moments(outer(t, LX, 3), c), sums)

    load_c.wait()
    pltpu.make_async_copy(cs.at[pl.ds(1, NP - 1)], cs.at[pl.ds(1, NP - 1)], c_recv).wait()
    every = cs[...]
    mine = cs[0]
    gap = every - mine[None]
    near = jnp.sum(jnp.sum(gap * gap, axis=1), axis=1, keepdims=True)
    center = jnp.sum(every, axis=0) * (1.0 / NP)
    off = every - center[None]
    spread = jnp.sum(jnp.sum(off * off, axis=0), keepdims=True) * (2.0 / (NP - 1))
    lane32 = lax.broadcasted_iota(jnp.int32, (NP, NG), 1)
    diag = lane32 == lax.broadcasted_iota(jnp.int32, (NP, NG), 0)
    near_row = jnp.sum(jnp.where(diag, near, 0.0), axis=0, keepdims=True)
    near_row = jnp.where(lane32[0:1] == NP, spread, near_row)

    m3 = sums[3] * tau
    rows = [jnp.sum(m, axis=0, keepdims=True) for m in (sums[0], sums[1], sums[2], m3)]
    blank = jnp.zeros((2, NG), F32)
    mom[0] = jnp.concatenate(rows + [jnp.broadcast_to(tau, (1, NG)), near_row, blank], axis=0)

    def send_m(r, carry):
        remote(mom.at[0], mom.at[NS - r], m_send, m_recv, peer_s(r)).start()
        return carry

    lax.fori_loop(1, NS, send_m, 0)
    pltpu.make_async_copy(mom.at[pl.ds(1, NS - 1)], mom.at[pl.ds(1, NS - 1)], m_recv).wait()

    taus = mom[:, 4:5, :]
    least = jnp.min(taus, axis=0)
    ratio = least[None] / taus
    q0 = jnp.sum(jnp.sum(mom[:, 0:1, :], axis=0), axis=1, keepdims=True)
    q1 = jnp.sum(jnp.sum(mom[:, 1:2, :] * ratio, axis=0), axis=1, keepdims=True)
    q2 = jnp.sum(jnp.sum(mom[:, 2:3, :] * ratio * ratio, axis=0), axis=1, keepdims=True)
    q3 = jnp.sum(jnp.sum(mom[:, 3:4, :] * ratio * ratio * ratio, axis=0), axis=1, keepdims=True)
    alpha = q0 / q1
    norm = alpha * alpha * q2 - q0
    grown = norm / q0 + 1.0
    alpha1 = norm / (alpha * alpha * (q3 - q2 * (q2 / q1)))
    tau0 = least[:, 0:1]
    scale0 = tau0 * (alpha + alpha1 * grown)
    scale1 = -(tau0 * alpha1) * (alpha * (tau0 / tau))

    def put_x(e, carry):
        xo[e] = xe[e + 2] + scale0 * u0[e + 1] + scale1 * u1[e]
        return carry

    lax.fori_loop(0, LX + 2, put_x, 0)
    store = pltpu.make_async_copy(xo.at[pl.ds(1, LX)], adj_hbm, out_sem)
    store.start()

    @pl.when(jnp.logical_not(first))
    def _():
        p_up().wait_recv()

    @pl.when(jnp.logical_not(last))
    def _():
        p_down().wait_recv()

    lhs_p = jnp.concatenate(
        [jnp.concatenate([byt[0], byt[0]], axis=1), jnp.concatenate([byt[1], byt[1]], axis=1)], axis=0
    )

    def cell_grad(x):
        a, p = xo[x + 1], pe[x + 1]
        upper = jnp.where(jnp.logical_and(last, x == LX - 1), 1.0, 0.5)
        lower = jnp.where(jnp.logical_and(first, x == 0), 1.0, 0.5)
        total = rim * (a * p)
        total = total + upper * ((xo[x + 2] - a) * (pe[x + 2] - p))
        total = total + lower * ((a - xo[x]) * (p - pe[x]))
        qy = inner_y * ((pltpu.roll(a, NG - 1, 0) - a) * (pltpu.roll(p, NG - 1, 0) - p))
        total = total + (qy + pltpu.roll(qy, 1, 0))
        qz = inner_z * ((pltpu.roll(a, NG - 1, 1) - a) * (pltpu.roll(p, NG - 1, 1) - p))
        total = total + (qz + pltpu.roll(qz, 1, 1))
        return jnp.concatenate(pieces(kp[x + HALO] * total, 2), axis=0)

    def proj_layers(t, carry):
        x = 2 * t
        got = mm(lhs_p, jnp.concatenate([cell_grad(x), cell_grad(x + 1)], axis=1))
        got = got[:M] + got[M:]
        pbuf[x] = got[:, :NG]
        pbuf[x + 1] = got[:, NG:]
        return carry

    lax.fori_loop(0, LX // 2, proj_layers, 0)

    def mix_x(i, carry):
        total = bx_ref[s * LX, i] * pbuf[0]
        for x in range(1, LX):
            total = total + bx_ref[s * LX + x, i] * pbuf[x]
        qbuf[i] = total
        return carry

    lax.fori_loop(0, M, mix_x, 0)
    q_two = jnp.concatenate(pieces(qbuf[...].reshape(M * M, NG), 2), axis=1)
    lhs_z = jnp.concatenate(
        [jnp.concatenate([bzt[0], bzt[0]], axis=1), jnp.concatenate([bzt[1], bzt[1]], axis=1)], axis=0
    )
    tensor = mm_nt(lhs_z, q_two)
    tensor = tensor[:M] + tensor[M:]
    rhs = jnp.concatenate(pieces(tensor, 3), axis=0)

    def share_out(r, carry):
        share = lax.rem(s + r, NS)
        cols = pl.ds(pl.multiple_of(share * SH, SH), SH)
        got = mm(rhs, hot[:, cols])
        got = (got[:M] + got[M : 2 * M] + got[2 * M :]) * lhot[:, cols]
        row = jnp.sum(got, axis=0, keepdims=True)
        for q in range(SH // NG):
            pk[r, q : q + 1, :] = row[:, q * NG : (q + 1) * NG]
        return carry

    def share_send(r, carry):
        share_out(r, carry)
        remote(pk.at[r], rp.at[NS - r], r_send, r_recv, peer_s(r)).start()
        return carry

    lax.fori_loop(1, NS, share_send, 0)
    share_out(0, 0)

    near_all = jnp.sum(mom[:, 5:6, :], axis=0)
    width = near_all[:, NP : NP + 1]
    kern = jnp.exp(-near_all / width)
    kcol = jnp.sum(jnp.where(diag, kern, 0.0), axis=1, keepdims=True)
    weight = jnp.broadcast_to(kcol[:, :, None], (NP, 1, NG))
    drive = jnp.sum(weight * every, axis=0)
    repel = jnp.sum(weight * (mine[None] - every), axis=0)
    base = mine + (STEP / NP) * ((2.0 / width) * repel - drive)

    pltpu.make_async_copy(rp.at[pl.ds(1, NS - 1)], rp.at[pl.ds(1, NS - 1)], r_recv).wait()
    total = pk[0]
    for r in range(1, NS):
        total = total + rp[r]
    gs[0] = total

    def send_g(r, carry):
        remote(gs.at[0], gs.at[NP - r], g_send, g_recv, peer_p(r)).start()
        return carry

    lax.fori_loop(1, NP, send_g, 0)
    pltpu.make_async_copy(gs.at[pl.ds(1, NP - 1)], gs.at[pl.ds(1, NP - 1)], g_recv).wait()
    new_ref[...] = base - (STEP / NP) * jnp.sum(weight * gs[...], axis=0)

    def sent(ref, sem):
        pltpu.make_async_copy(ref, ref, sem).wait()

    sent(cs.at[pl.ds(1, NP - 1)], c_send)
    sent(mom.at[pl.ds(1, NS - 1)], m_send)
    sent(rp.at[pl.ds(1, NS - 1)], r_send)
    sent(gs.at[pl.ds(1, NP - 1)], g_send)

    @pl.when(jnp.logical_not(last))
    def _():
        x_up().wait_send()
        p_up().wait_send()
        r_up().wait_send()

    @pl.when(jnp.logical_not(first))
    def _():
        x_down().wait_send()
        p_down().wait_send()
        r_down().wait_send()

    store.wait()


def shards(coeffs, modes, basis_x, basis_y, basis_z, pressure, initial_adjoint, sensors, observed, precision):
    vmem = pl.BlockSpec(memory_space=pltpu.VMEM)
    smem = pl.BlockSpec(memory_space=pltpu.SMEM)
    anywhere = pl.BlockSpec(memory_space=pl.ANY)
    dma = pltpu.SemaphoreType.DMA
    layers = lambda count: pltpu.VMEM((count, NG, NG), F32)
    new, adjoint = pl.pallas_call(
        kernel,
        out_shape=(
            jax.ShapeDtypeStruct((SH // NG, NG), F32),
            jax.ShapeDtypeStruct((LX, NG, NG), F32),
        ),
        in_specs=[anywhere, vmem, smem, vmem, vmem, anywhere, anywhere, smem, smem, smem],
        out_specs=(vmem, anywhere),
        scratch_shapes=[
            layers(LX + 6),
            layers(LX + 2),
            layers(LX + 6),
            layers(LX + 6),
            layers(LX + 6),
            layers(LX + 6),
            layers(LX + 6),
            layers(LX + 4),
            layers(LX + 2),
            layers(LX + 2),
            pltpu.VMEM((LX + 4, 8, NG), F32),
            pltpu.VMEM((M * M, K), BF16),
            pltpu.VMEM((M, K), F32),
            pltpu.VMEM((3 * M, K), BF16),
            pltpu.VMEM((NG, NG), F32),
            pltpu.VMEM((M, M, NG), F32),
            pltpu.VMEM((LX, M, NG), F32),
            pltpu.VMEM((M, M, NG), F32),
            pltpu.VMEM((NP, SH // NG, NG), F32),
            pltpu.VMEM((NS, SH // NG, NG), F32),
            pltpu.VMEM((NS, SH // NG, NG), F32),
            pltpu.VMEM((NS, SH // NG, NG), F32),
            pltpu.VMEM((NP, SH // NG, NG), F32),
            pltpu.VMEM((NS, 8, NG), F32),
            dma((3,)), dma, dma((6,)), dma((6,)),
            dma, dma, dma, dma, dma, dma, dma, dma, dma,
        ],
        compiler_params=pltpu.CompilerParams(
            collective_id=0, has_side_effects=True, vmem_limit_bytes=48 * 2**20
        ),
    )(
        coeffs.reshape(NS, SH // NG, NG),
        modes.reshape(K // NG, NG),
        basis_x,
        basis_y,
        basis_z,
        pressure[0],
        initial_adjoint[0],
        sensors,
        observed,
        precision,
    )
    return new.reshape(1, SH), adjoint[None]


def solution(mesh):
    in_specs = (
        P("particle", None),
        P(),
        P(),
        P(),
        P(),
        P("particle", "space", None, None),
        P("particle", "space", None, None),
        P(),
        P(),
        P(),
    )
    out_specs = (P("particle", "space"), P("particle", "space", None, None))
    return jax.shard_map(shards, mesh=mesh, in_specs=in_specs, out_specs=out_specs, check_vma=False)
```

```python
import jax
import jax.numpy as jnp
from jax import lax
from jax.experimental import pallas as pl
from jax.experimental.pallas import tpu as pltpu
from jax.sharding import PartitionSpec as P

F32 = jnp.float32
BF16 = jnp.bfloat16
NP = 32
NS = 8
LX = 16
NX = 128
NG = 128
M = 16
K = M * M * M
SH = K // NS
HALO = 3
STEP = 0.5
NN = (((1,), (1,)), ((), ()))


def pieces(value, count):
    out = []
    rest = value
    for _ in range(count):
        part = rest.astype(BF16)
        out.append(part)
        rest = rest - part.astype(F32)
    return out


def mm(a, b):
    return jnp.dot(a, b, preferred_element_type=F32)


def mm_nt(a, b):
    return lax.dot_general(a, b, NN, preferred_element_type=F32)


def fold(value):
    return jnp.sum(value.reshape(NG // 8, 8, NG), axis=0)


def kernel(
    c_hbm, modes_ref, bx_ref, by_ref, bz_ref, p_hbm, x_hbm, sens_ref, obs_ref, prec_ref,
    new_ref, adj_hbm,
    xe, pe, kp, kx, ky, kz, kb, u0, u1, xo, rsum, hot, lhot, lcs, fbuf, pbuf, qbuf,
    cs, wk, pk, rp, gs, mom,
    in_sem, out_sem, halo_send, halo_recv, c_own, c_send, c_recv, m_send, m_recv, r_send, r_recv, g_send, g_recv,
):
    n = lax.axis_index("particle")
    s = lax.axis_index("space")
    first = s == 0
    last = s == NS - 1

    def peer_p(r):
        return {"particle": lax.rem(n + r, NP)}

    def peer_s(r):
        return {"space": lax.rem(s + r, NS)}

    barrier = pltpu.get_barrier_semaphore()

    def greet_s(r, carry):
        pl.semaphore_signal(barrier, inc=1, device_id=peer_s(r))
        return carry

    def greet_p(r, carry):
        pl.semaphore_signal(barrier, inc=1, device_id=peer_p(r))
        return carry

    lax.fori_loop(1, NS, greet_s, 0)
    lax.fori_loop(1, NP, greet_p, 0)

    load_x = pltpu.make_async_copy(x_hbm, xe.at[pl.ds(HALO, LX)], in_sem.at[0])
    load_p = pltpu.make_async_copy(p_hbm, pe.at[pl.ds(1, LX)], in_sem.at[1])
    load_c = pltpu.make_async_copy(c_hbm.at[s], cs.at[0], c_own)
    load_all = pltpu.make_async_copy(c_hbm, wk, in_sem.at[2])
    load_all.start()
    load_p.start()
    load_x.start()
    load_c.start()

    load_all.wait()
    row_id = lax.broadcasted_iota(jnp.int32, (M * M, NG), 0)
    sub_id = lax.broadcasted_iota(jnp.int32, (M, NG), 0)
    for chunk in range(K // NG):
        pos = modes_ref[chunk : chunk + 1, :]
        cols = slice(chunk * NG, (chunk + 1) * NG)
        upper = lax.shift_right_logical(pos, 4)
        lower = lax.bitwise_and(pos, 15)
        hot[:, cols] = jnp.where(row_id == upper, 1.0, 0.0).astype(BF16)
        low = jnp.where(sub_id == lower, 1.0, 0.0)
        lhot[:, cols] = low
        own = wk[chunk // 4, chunk % 4 : chunk % 4 + 1, :]
        for q, part in enumerate(pieces(own, 3)):
            lcs[q * M : (q + 1) * M, cols] = (low * part.astype(F32)).astype(BF16)

    pl.semaphore_wait(barrier, NS - 1 + NP - 1)

    up = {"space": jnp.minimum(s + 1, NS - 1)}
    down = {"space": jnp.maximum(s - 1, 0)}

    def remote(src, dst, send, recv, where):
        return pltpu.make_async_remote_copy(src_ref=src, dst_ref=dst, send_sem=send, recv_sem=recv, device_id=where)

    def x_up():
        return remote(x_hbm.at[pl.ds(LX - HALO, HALO)], xe.at[pl.ds(0, HALO)], halo_send.at[0], halo_recv.at[0], up)

    def x_down():
        return remote(x_hbm.at[pl.ds(0, HALO)], xe.at[pl.ds(HALO + LX, HALO)], halo_send.at[1], halo_recv.at[1], down)

    def p_up():
        return remote(p_hbm.at[pl.ds(LX - 1, 1)], pe.at[pl.ds(0, 1)], halo_send.at[2], halo_recv.at[2], up)

    def p_down():
        return remote(p_hbm.at[pl.ds(0, 1)], pe.at[pl.ds(LX + 1, 1)], halo_send.at[3], halo_recv.at[3], down)

    def r_up():
        return remote(rsum.at[pl.ds(LX, 2)], rsum.at[pl.ds(0, 2)], halo_send.at[4], halo_recv.at[4], up)

    def r_down():
        return remote(rsum.at[pl.ds(2, 2)], rsum.at[pl.ds(LX + 2, 2)], halo_send.at[5], halo_recv.at[5], down)

    @pl.when(jnp.logical_not(last))
    def _():
        x_up().start()

    @pl.when(jnp.logical_not(first))
    def _():
        x_down().start()

    @pl.when(jnp.logical_not(last))
    def _():
        p_up().start()

    @pl.when(jnp.logical_not(first))
    def _():
        p_down().start()

    def send_c(r, carry):
        remote(c_hbm.at[s], cs.at[NP - r], c_send, c_recv, peer_p(r)).start()
        return carry

    lax.fori_loop(1, NP, send_c, 0)

    @pl.when(first)
    def _():
        xe[0:HALO] = jnp.zeros((HALO, NG, NG), F32)
        pe[0:1] = jnp.zeros((1, NG, NG), F32)
        rsum[0:2] = jnp.zeros((2, 8, NG), F32)

    @pl.when(last)
    def _():
        xe[HALO + LX :] = jnp.zeros((HALO, NG, NG), F32)
        pe[LX + 1 :] = jnp.zeros((1, NG, NG), F32)
        rsum[LX + 2 :] = jnp.zeros((2, 8, NG), F32)

    flat = (
        lax.broadcasted_iota(jnp.int32, (M, NG), 0) * NG + lax.broadcasted_iota(jnp.int32, (M, NG), 1)
    )

    def sensor_of(layer, block):
        index = layer * 8 + block
        return index, sens_ref[index] - index * (M * NG)

    load_p.wait()

    def misfit(x, carry):
        for b in range(8):
            index, cell = sensor_of(s * LX + x, b)
            part = pe[x + 1, b * M : (b + 1) * M, :]
            hit = jnp.where(flat == cell, (part - obs_ref[index]) * prec_ref[index], 0.0)
            rsum[x + 2, b : b + 1, :] = jnp.sum(hit, axis=0, keepdims=True)
        return carry

    lax.fori_loop(0, LX, misfit, 0)

    @pl.when(jnp.logical_not(last))
    def _():
        r_up().start()

    @pl.when(jnp.logical_not(first))
    def _():
        r_down().start()

    lane = lax.broadcasted_iota(jnp.int32, (NG, NG), 1)
    suby = lax.broadcasted_iota(jnp.int32, (NG, NG), 0)
    eye = jnp.where(lane == suby, 1.0, 0.0).astype(BF16)
    byt = pieces(by_ref[...], 3)
    bzt = pieces(bz_ref[...], 3)
    lhs_y = mm_nt(eye, jnp.concatenate([byt[which] for which in (0, 0, 1, 0, 1, 2)], axis=0)).astype(BF16)

    xi = mm_nt(hot[...], lcs[...]).astype(BF16)
    field = mm(xi, jnp.concatenate([bzt[0]] * 3, axis=0))
    field = field + mm(xi, jnp.concatenate([bzt[1]] * 3, axis=0))
    field = field + mm(xi, jnp.concatenate([bzt[2]] * 3, axis=0))
    fbuf[...] = field.reshape(M, M, NG)

    inner_y = jnp.where(suby == NG - 1, 0.0, 0.5)
    inner_z = jnp.where(lane == NG - 1, 0.0, 0.5)
    rim = (
        jnp.where(suby == NG - 1, 1.0, 0.0)
        + jnp.where(suby == 0, 1.0, 0.0)
        + jnp.where(lane == NG - 1, 1.0, 0.0)
        + jnp.where(lane == 0, 1.0, 0.0)
    )

    def mix(e):
        g = jnp.clip(s * LX - HALO + e, 0, NX - 1)
        total = bx_ref[0, g] * fbuf[0]
        for i in range(1, M):
            total = total + bx_ref[i, g] * fbuf[i]
        a, b, c = pieces(total, 3)
        return jnp.concatenate([a, b, a, c, b, a], axis=0)

    def faces(e, k, before):
        kp[e] = k
        ky[e] = inner_y * (k + pltpu.roll(k, NG - 1, 0))
        kz[e] = inner_z * (k + pltpu.roll(k, NG - 1, 1))
        kb[e] = rim * k
        kx[before] = 0.5 * (kp[before] + k)

    def log_layers(t, top):
        e = 2 * t
        both = jnp.exp(mm(lhs_y, jnp.concatenate([mix(e), mix(e + 1)], axis=1)))
        k0, k1 = both[:, :NG], both[:, NG:]
        faces(e, k0, jnp.maximum(e - 1, 0))
        faces(e + 1, k1, e)
        return jnp.maximum(top, jnp.max(jnp.maximum(k0, k1).reshape(NG // 8, 8, NG), axis=0))

    top = lax.fori_loop(0, HALO + LX // 2, log_layers, jnp.zeros((8, NG), F32))
    tau = (1.0 / 16.0) / jnp.max(top, keepdims=True)

    def apply(v_ref, i, e):
        v = v_ref[i]
        total = kb[e] * v
        total = total - kx[e] * (v_ref[i + 1] - v)
        total = total + kx[e - 1] * (v - v_ref[i - 1])
        fy = ky[e] * (pltpu.roll(v, NG - 1, 0) - v)
        total = total - (fy - pltpu.roll(fy, 1, 0))
        fz = kz[e] * (pltpu.roll(v, NG - 1, 1) - v)
        total = total - (fz - pltpu.roll(fz, 1, 1))
        return v, total

    def inside(g):
        return jnp.where(jnp.logical_and(g >= 0, g < NX), 1, 0)

    def put_u0(e):
        g = s * LX - 2 + e
        safe = jnp.clip(g, 0, NX - 1)
        _, image = apply(xe, e + 1, e + 1)
        load = []
        for b in range(8):
            _, cell = sensor_of(safe, b)
            load.append(jnp.where(flat == cell, rsum[e, b : b + 1, :], 0.0))
        value = jnp.concatenate(load, axis=0) - image
        u0[e] = jnp.where(inside(g) == 1, value, 0.0)

    def put_u1(e):
        g = s * LX - 1 + e
        _, image = apply(u0, e + 1, e + 2)
        u1[e] = jnp.where(inside(g) == 1, image * tau, 0.0)

    def moments(x, sums):
        second, image = apply(u1, x + 1, x + 3)
        start = u0[x + 2]
        m0, m1, m2, m3 = sums
        return (
            m0 + fold(start * start),
            m1 + fold(start * second),
            m2 + fold(second * second),
            m3 + fold(second * image),
        )

    def outer(t, count, width):
        return t + jnp.where(t >= width, count - 2 * width, 0)

    load_x.wait()
    lax.fori_loop(3, 17, lambda e, c: (put_u0(e), c)[1], 0)
    lax.fori_loop(3, 15, lambda e, c: (put_u1(e), c)[1], 0)
    zero = jnp.zeros((8, NG), F32)
    sums = lax.fori_loop(3, 13, moments, (zero, zero, zero, zero))

    @pl.when(jnp.logical_not(first))
    def _():
        x_up().wait_recv()
        r_up().wait_recv()

    @pl.when(jnp.logical_not(last))
    def _():
        x_down().wait_recv()
        r_down().wait_recv()

    lax.fori_loop(0, 6, lambda t, c: (put_u0(outer(t, LX + 4, 3)), c)[1], 0)
    lax.fori_loop(0, 6, lambda t, c: (put_u1(outer(t, LX + 2, 3)), c)[1], 0)
    sums = lax.fori_loop(0, 6, lambda t, c: moments(outer(t, LX, 3), c), sums)

    load_c.wait()
    pltpu.make_async_copy(cs.at[pl.ds(1, NP - 1)], cs.at[pl.ds(1, NP - 1)], c_recv).wait()
    every = cs[...]
    mine = cs[0]
    gap = every - mine[None]
    near = jnp.sum(jnp.sum(gap * gap, axis=1), axis=1, keepdims=True)
    center = jnp.sum(every, axis=0) * (1.0 / NP)
    off = every - center[None]
    spread = jnp.sum(jnp.sum(off * off, axis=0), keepdims=True) * (2.0 / (NP - 1))
    lane32 = lax.broadcasted_iota(jnp.int32, (NP, NG), 1)
    diag = lane32 == lax.broadcasted_iota(jnp.int32, (NP, NG), 0)
    near_row = jnp.sum(jnp.where(diag, near, 0.0), axis=0, keepdims=True)
    near_row = jnp.where(lane32[0:1] == NP, spread, near_row)

    m3 = sums[3] * tau
    rows = [jnp.sum(m, axis=0, keepdims=True) for m in (sums[0], sums[1], sums[2], m3)]
    blank = jnp.zeros((2, NG), F32)
    mom[0] = jnp.concatenate(rows + [jnp.broadcast_to(tau, (1, NG)), near_row, blank], axis=0)

    def send_m(r, carry):
        remote(mom.at[0], mom.at[NS - r], m_send, m_recv, peer_s(r)).start()
        return carry

    lax.fori_loop(1, NS, send_m, 0)
    pltpu.make_async_copy(mom.at[pl.ds(1, NS - 1)], mom.at[pl.ds(1, NS - 1)], m_recv).wait()

    taus = mom[:, 4:5, :]
    least = jnp.min(taus, axis=0)
    ratio = least[None] / taus
    q0 = jnp.sum(jnp.sum(mom[:, 0:1, :], axis=0), axis=1, keepdims=True)
    q1 = jnp.sum(jnp.sum(mom[:, 1:2, :] * ratio, axis=0), axis=1, keepdims=True)
    q2 = jnp.sum(jnp.sum(mom[:, 2:3, :] * ratio * ratio, axis=0), axis=1, keepdims=True)
    q3 = jnp.sum(jnp.sum(mom[:, 3:4, :] * ratio * ratio * ratio, axis=0), axis=1, keepdims=True)
    alpha = q0 / q1
    norm = alpha * alpha * q2 - q0
    grown = norm / q0 + 1.0
    alpha1 = norm / (alpha * alpha * (q3 - q2 * (q2 / q1)))
    tau0 = least[:, 0:1]
    scale0 = tau0 * (alpha + alpha1 * grown)
    scale1 = -(tau0 * alpha1) * (alpha * (tau0 / tau))

    def put_x(e, carry):
        xo[e] = xe[e + 2] + scale0 * u0[e + 1] + scale1 * u1[e]
        return carry

    lax.fori_loop(0, LX + 2, put_x, 0)
    store = pltpu.make_async_copy(xo.at[pl.ds(1, LX)], adj_hbm, out_sem)
    store.start()

    @pl.when(jnp.logical_not(first))
    def _():
        p_up().wait_recv()

    @pl.when(jnp.logical_not(last))
    def _():
        p_down().wait_recv()

    lhs_p = jnp.concatenate(
        [jnp.concatenate([byt[0], byt[0]], axis=1), jnp.concatenate([byt[1], byt[1]], axis=1)], axis=0
    )

    def cell_grad(x):
        a, p = xo[x + 1], pe[x + 1]
        upper = jnp.where(jnp.logical_and(last, x == LX - 1), 1.0, 0.5)
        lower = jnp.where(jnp.logical_and(first, x == 0), 1.0, 0.5)
        total = rim * (a * p)
        total = total + upper * ((xo[x + 2] - a) * (pe[x + 2] - p))
        total = total + lower * ((a - xo[x]) * (p - pe[x]))
        qy = inner_y * ((pltpu.roll(a, NG - 1, 0) - a) * (pltpu.roll(p, NG - 1, 0) - p))
        total = total + (qy + pltpu.roll(qy, 1, 0))
        qz = inner_z * ((pltpu.roll(a, NG - 1, 1) - a) * (pltpu.roll(p, NG - 1, 1) - p))
        total = total + (qz + pltpu.roll(qz, 1, 1))
        return jnp.concatenate(pieces(kp[x + HALO] * total, 2), axis=0)

    def proj_layers(t, carry):
        x = 2 * t
        got = mm(lhs_p, jnp.concatenate([cell_grad(x), cell_grad(x + 1)], axis=1))
        got = got[:M] + got[M:]
        pbuf[x] = got[:, :NG]
        pbuf[x + 1] = got[:, NG:]
        return carry

    lax.fori_loop(0, LX // 2, proj_layers, 0)

    def mix_x(i, carry):
        total = bx_ref[i, s * LX] * pbuf[0]
        for x in range(1, LX):
            total = total + bx_ref[i, s * LX + x] * pbuf[x]
        qbuf[i] = total
        return carry

    lax.fori_loop(0, M, mix_x, 0)
    q_two = jnp.concatenate(pieces(qbuf[...].reshape(M * M, NG), 2), axis=1)
    lhs_z = jnp.concatenate(
        [jnp.concatenate([bzt[0], bzt[0]], axis=1), jnp.concatenate([bzt[1], bzt[1]], axis=1)], axis=0
    )
    tensor = mm_nt(lhs_z, q_two)
    tensor = tensor[:M] + tensor[M:]
    rhs = jnp.concatenate(pieces(tensor, 3), axis=0)

    def share_out(r, carry):
        share = lax.rem(s + r, NS)
        cols = pl.ds(pl.multiple_of(share * SH, SH), SH)
        got = mm(rhs, hot[:, cols])
        got = (got[:M] + got[M : 2 * M] + got[2 * M :]) * lhot[:, cols]
        row = jnp.sum(got, axis=0, keepdims=True)
        for q in range(SH // NG):
            pk[r, q : q + 1, :] = row[:, q * NG : (q + 1) * NG]
        return carry

    def share_send(r, carry):
        share_out(r, carry)
        remote(pk.at[r], rp.at[NS - r], r_send, r_recv, peer_s(r)).start()
        return carry

    lax.fori_loop(1, NS, share_send, 0)
    share_out(0, 0)

    near_all = jnp.sum(mom[:, 5:6, :], axis=0)
    width = near_all[:, NP : NP + 1]
    kern = jnp.exp(-near_all / width)
    kcol = jnp.sum(jnp.where(diag, kern, 0.0), axis=1, keepdims=True)
    weight = jnp.broadcast_to(kcol[:, :, None], (NP, 1, NG))
    drive = jnp.sum(weight * every, axis=0)
    repel = jnp.sum(weight * (mine[None] - every), axis=0)
    base = mine + (STEP / NP) * ((2.0 / width) * repel - drive)

    pltpu.make_async_copy(rp.at[pl.ds(1, NS - 1)], rp.at[pl.ds(1, NS - 1)], r_recv).wait()
    total = pk[0]
    for r in range(1, NS):
        total = total + rp[r]
    gs[0] = total

    def send_g(r, carry):
        remote(gs.at[0], gs.at[NP - r], g_send, g_recv, peer_p(r)).start()
        return carry

    lax.fori_loop(1, NP, send_g, 0)
    pltpu.make_async_copy(gs.at[pl.ds(1, NP - 1)], gs.at[pl.ds(1, NP - 1)], g_recv).wait()
    new_ref[...] = base - (STEP / NP) * jnp.sum(weight * gs[...], axis=0)

    def sent(ref, sem):
        pltpu.make_async_copy(ref, ref, sem).wait()

    sent(cs.at[pl.ds(1, NP - 1)], c_send)
    sent(mom.at[pl.ds(1, NS - 1)], m_send)
    sent(rp.at[pl.ds(1, NS - 1)], r_send)
    sent(gs.at[pl.ds(1, NP - 1)], g_send)

    @pl.when(jnp.logical_not(last))
    def _():
        x_up().wait_send()
        p_up().wait_send()
        r_up().wait_send()

    @pl.when(jnp.logical_not(first))
    def _():
        x_down().wait_send()
        p_down().wait_send()
        r_down().wait_send()

    store.wait()


def shards(coeffs, modes, basis_x, basis_y, basis_z, pressure, initial_adjoint, sensors, observed, precision):
    vmem = pl.BlockSpec(memory_space=pltpu.VMEM)
    smem = pl.BlockSpec(memory_space=pltpu.SMEM)
    anywhere = pl.BlockSpec(memory_space=pl.ANY)
    dma = pltpu.SemaphoreType.DMA
    layers = lambda count: pltpu.VMEM((count, NG, NG), F32)
    new, adjoint = pl.pallas_call(
        kernel,
        out_shape=(
            jax.ShapeDtypeStruct((SH // NG, NG), F32),
            jax.ShapeDtypeStruct((LX, NG, NG), F32),
        ),
        in_specs=[anywhere, vmem, smem, vmem, vmem, anywhere, anywhere, smem, smem, smem],
        out_specs=(vmem, anywhere),
        scratch_shapes=[
            layers(LX + 6),
            layers(LX + 2),
            layers(LX + 6),
            layers(LX + 6),
            layers(LX + 6),
            layers(LX + 6),
            layers(LX + 6),
            layers(LX + 4),
            layers(LX + 2),
            layers(LX + 2),
            pltpu.VMEM((LX + 4, 8, NG), F32),
            pltpu.VMEM((M * M, K), BF16),
            pltpu.VMEM((M, K), F32),
            pltpu.VMEM((3 * M, K), BF16),
            pltpu.VMEM((M, M, NG), F32),
            pltpu.VMEM((LX, M, NG), F32),
            pltpu.VMEM((M, M, NG), F32),
            pltpu.VMEM((NP, SH // NG, NG), F32),
            pltpu.VMEM((NS, SH // NG, NG), F32),
            pltpu.VMEM((NS, SH // NG, NG), F32),
            pltpu.VMEM((NS, SH // NG, NG), F32),
            pltpu.VMEM((NP, SH // NG, NG), F32),
            pltpu.VMEM((NS, 8, NG), F32),
            dma((3,)), dma, dma((6,)), dma((6,)),
            dma, dma, dma, dma, dma, dma, dma, dma, dma,
        ],
        compiler_params=pltpu.CompilerParams(
            collective_id=0, has_side_effects=True, vmem_limit_bytes=60 * 2**20
        ),
    )(
        coeffs.reshape(NS, SH // NG, NG),
        modes.reshape(K // NG, NG),
        basis_x.T,
        basis_y.T,
        basis_z.T,
        pressure[0],
        initial_adjoint[0],
        sensors,
        observed,
        precision,
    )
    return new.reshape(1, SH), adjoint[None]


def solution(mesh):
    in_specs = (
        P("particle", None),
        P(),
        P(),
        P(),
        P(),
        P("particle", "space", None, None),
        P("particle", "space", None, None),
        P(),
        P(),
        P(),
    )
    out_specs = (P("particle", "space"), P("particle", "space", None, None))
    return jax.shard_map(shards, mesh=mesh, in_specs=in_specs, out_specs=out_specs, check_vma=False)
```

```python
import jax
import jax.numpy as jnp
from jax import lax
from jax.experimental import pallas as pl
from jax.experimental.pallas import tpu as pltpu
from jax.sharding import PartitionSpec as P

F32 = jnp.float32
BF16 = jnp.bfloat16
NP = 32
NS = 8
LX = 16
NX = 128
NG = 128
M = 16
K = M * M * M
SH = K // NS
HALO = 3
STEP = 0.5
NN = (((1,), (1,)), ((), ()))


def pieces(value, count):
    out = []
    rest = value
    for _ in range(count):
        part = rest.astype(BF16)
        out.append(part)
        rest = rest - part.astype(F32)
    return out


def mm(a, b):
    return jnp.dot(a, b, preferred_element_type=F32)


def mm_nt(a, b):
    return lax.dot_general(a, b, NN, preferred_element_type=F32)


def fold(value):
    return jnp.sum(value.reshape(NG // 8, 8, NG), axis=0)


def kernel(
    c_hbm, modes_ref, bx_ref, by_ref, bz_ref, p_hbm, x_hbm, sens_ref, obs_ref, prec_ref,
    new_ref, adj_hbm,
    xe, pe, kp, kx, ky, kz, kb, u0, u1, xo, rsum, hot, lhot, lcs, fbuf, pbuf, qbuf,
    cs, wk, pk, rp, gs,
    in_sem, out_sem, halo_send, halo_recv, c_own, c_send, c_recv, r_send, r_recv, g_send, g_recv,
):
    n = lax.axis_index("particle")
    s = lax.axis_index("space")
    first = s == 0
    last = s == NS - 1

    def peer_p(r):
        return {"particle": lax.rem(n + r, NP)}

    def peer_s(r):
        return {"space": lax.rem(s + r, NS)}

    barrier = pltpu.get_barrier_semaphore()

    def greet_s(r, carry):
        pl.semaphore_signal(barrier, inc=1, device_id=peer_s(r))
        return carry

    def greet_p(r, carry):
        pl.semaphore_signal(barrier, inc=1, device_id=peer_p(r))
        return carry

    lax.fori_loop(1, NS, greet_s, 0)
    lax.fori_loop(1, NP, greet_p, 0)

    load_x = pltpu.make_async_copy(x_hbm, xe.at[pl.ds(HALO, LX)], in_sem.at[0])
    load_p = pltpu.make_async_copy(p_hbm, pe.at[pl.ds(1, LX)], in_sem.at[1])
    load_c = pltpu.make_async_copy(c_hbm.at[s], cs.at[0], c_own)
    load_all = pltpu.make_async_copy(c_hbm, wk, in_sem.at[2])
    load_all.start()
    load_p.start()
    load_x.start()
    load_c.start()

    load_all.wait()
    row_id = lax.broadcasted_iota(jnp.int32, (M * M, NG), 0)
    sub_id = lax.broadcasted_iota(jnp.int32, (M, NG), 0)
    for chunk in range(K // NG):
        pos = modes_ref[chunk : chunk + 1, :]
        cols = slice(chunk * NG, (chunk + 1) * NG)
        upper = lax.shift_right_logical(pos, 4)
        lower = lax.bitwise_and(pos, 15)
        hot[:, cols] = jnp.where(row_id == upper, 1.0, 0.0).astype(BF16)
        low = jnp.where(sub_id == lower, 1.0, 0.0)
        lhot[:, cols] = low
        own = wk[chunk // 4, chunk % 4 : chunk % 4 + 1, :]
        for q, part in enumerate(pieces(own, 3)):
            lcs[q * M : (q + 1) * M, cols] = (low * part.astype(F32)).astype(BF16)

    lane = lax.broadcasted_iota(jnp.int32, (NG, NG), 1)
    suby = lax.broadcasted_iota(jnp.int32, (NG, NG), 0)
    eye = jnp.where(lane == suby, 1.0, 0.0).astype(BF16)
    byt = pieces(by_ref[...], 3)
    bzt = pieces(bz_ref[...], 3)
    lhs_y = mm_nt(eye, jnp.concatenate([byt[which] for which in (0, 0, 1, 0, 1, 2)], axis=0)).astype(BF16)

    xi = mm_nt(hot[...], lcs[...]).astype(BF16)
    field = mm(xi, jnp.concatenate([bzt[0]] * 3, axis=0))
    field = field + mm(xi, jnp.concatenate([bzt[1]] * 3, axis=0))
    field = field + mm(xi, jnp.concatenate([bzt[2]] * 3, axis=0))
    fbuf[...] = field.reshape(M, M, NG)

    inner_y = jnp.where(suby == NG - 1, 0.0, 0.5)
    inner_z = jnp.where(lane == NG - 1, 0.0, 0.5)
    rim = (
        jnp.where(suby == NG - 1, 1.0, 0.0)
        + jnp.where(suby == 0, 1.0, 0.0)
        + jnp.where(lane == NG - 1, 1.0, 0.0)
        + jnp.where(lane == 0, 1.0, 0.0)
    )

    def mix(e):
        g = jnp.clip(s * LX - HALO + e, 0, NX - 1)
        total = bx_ref[0, g] * fbuf[0]
        for i in range(1, M):
            total = total + bx_ref[i, g] * fbuf[i]
        a, b, c = pieces(total, 3)
        return jnp.concatenate([a, b, a, c, b, a], axis=0)

    def faces(e, k, before):
        kp[e] = k
        ky[e] = inner_y * (k + pltpu.roll(k, NG - 1, 0))
        kz[e] = inner_z * (k + pltpu.roll(k, NG - 1, 1))
        kb[e] = rim * k
        kx[before] = 0.5 * (kp[before] + k)

    def log_layers(t, top):
        e = 2 * t
        both = jnp.exp(mm(lhs_y, jnp.concatenate([mix(e), mix(e + 1)], axis=1)))
        k0, k1 = both[:, :NG], both[:, NG:]
        faces(e, k0, jnp.maximum(e - 1, 0))
        faces(e + 1, k1, e)
        return jnp.maximum(top, jnp.max(jnp.maximum(k0, k1).reshape(NG // 8, 8, NG), axis=0))

    top = lax.fori_loop(0, HALO + LX // 2, log_layers, jnp.zeros((8, NG), F32))
    tau = (1.0 / 16.0) / jnp.max(top, keepdims=True)

    @pl.when(first)
    def _():
        xe[0:HALO] = jnp.zeros((HALO, NG, NG), F32)
        pe[0:1] = jnp.zeros((1, NG, NG), F32)
        rsum[0:2] = jnp.zeros((2, 8, NG), F32)

    @pl.when(last)
    def _():
        xe[HALO + LX :] = jnp.zeros((HALO, NG, NG), F32)
        pe[LX + 1 :] = jnp.zeros((1, NG, NG), F32)
        rsum[LX + 2 :] = jnp.zeros((2, 8, NG), F32)

    flat = (
        lax.broadcasted_iota(jnp.int32, (M, NG), 0) * NG + lax.broadcasted_iota(jnp.int32, (M, NG), 1)
    )

    def sensor_of(layer, block):
        index = layer * 8 + block
        return index, sens_ref[index] - index * (M * NG)

    load_p.wait()

    def misfit(x, carry):
        for b in range(8):
            index, cell = sensor_of(s * LX + x, b)
            part = pe[x + 1, b * M : (b + 1) * M, :]
            hit = jnp.where(flat == cell, (part - obs_ref[index]) * prec_ref[index], 0.0)
            rsum[x + 2, b : b + 1, :] = jnp.sum(hit, axis=0, keepdims=True)
        return carry

    lax.fori_loop(0, LX, misfit, 0)

    pl.semaphore_wait(barrier, NS - 1 + NP - 1)

    up = {"space": jnp.minimum(s + 1, NS - 1)}
    down = {"space": jnp.maximum(s - 1, 0)}

    def remote(src, dst, send, recv, where):
        return pltpu.make_async_remote_copy(src_ref=src, dst_ref=dst, send_sem=send, recv_sem=recv, device_id=where)

    def x_up():
        return remote(x_hbm.at[pl.ds(LX - HALO, HALO)], xe.at[pl.ds(0, HALO)], halo_send.at[0], halo_recv.at[0], up)

    def x_down():
        return remote(x_hbm.at[pl.ds(0, HALO)], xe.at[pl.ds(HALO + LX, HALO)], halo_send.at[1], halo_recv.at[1], down)

    def p_up():
        return remote(p_hbm.at[pl.ds(LX - 1, 1)], pe.at[pl.ds(0, 1)], halo_send.at[2], halo_recv.at[2], up)

    def p_down():
        return remote(p_hbm.at[pl.ds(0, 1)], pe.at[pl.ds(LX + 1, 1)], halo_send.at[3], halo_recv.at[3], down)

    def r_up():
        return remote(rsum.at[pl.ds(LX, 2)], rsum.at[pl.ds(0, 2)], halo_send.at[4], halo_recv.at[4], up)

    def r_down():
        return remote(rsum.at[pl.ds(2, 2)], rsum.at[pl.ds(LX + 2, 2)], halo_send.at[5], halo_recv.at[5], down)

    @pl.when(jnp.logical_not(last))
    def _():
        x_up().start()

    @pl.when(jnp.logical_not(first))
    def _():
        x_down().start()

    @pl.when(jnp.logical_not(last))
    def _():
        p_up().start()

    @pl.when(jnp.logical_not(first))
    def _():
        p_down().start()

    def send_c(r, carry):
        remote(c_hbm.at[s], cs.at[NP - r], c_send, c_recv, peer_p(r)).start()
        return carry

    @pl.when(jnp.logical_not(last))
    def _():
        r_up().start()

    @pl.when(jnp.logical_not(first))
    def _():
        r_down().start()

    lax.fori_loop(1, NP, send_c, 0)

    def apply(v_ref, i, e):
        v = v_ref[i]
        total = kb[e] * v
        total = total - kx[e] * (v_ref[i + 1] - v)
        total = total + kx[e - 1] * (v - v_ref[i - 1])
        fy = ky[e] * (pltpu.roll(v, NG - 1, 0) - v)
        total = total - (fy - pltpu.roll(fy, 1, 0))
        fz = kz[e] * (pltpu.roll(v, NG - 1, 1) - v)
        total = total - (fz - pltpu.roll(fz, 1, 1))
        return v, total

    def inside(g):
        return jnp.where(jnp.logical_and(g >= 0, g < NX), 1, 0)

    def put_u0(e):
        g = s * LX - 2 + e
        safe = jnp.clip(g, 0, NX - 1)
        _, image = apply(xe, e + 1, e + 1)
        load = []
        for b in range(8):
            _, cell = sensor_of(safe, b)
            load.append(jnp.where(flat == cell, rsum[e, b : b + 1, :], 0.0))
        value = jnp.concatenate(load, axis=0) - image
        u0[e] = jnp.where(inside(g) == 1, value, 0.0)

    def put_u1(e):
        g = s * LX - 1 + e
        _, image = apply(u0, e + 1, e + 2)
        u1[e] = jnp.where(inside(g) == 1, image * tau, 0.0)

    def moments(x, sums):
        second, image = apply(u1, x + 1, x + 3)
        start = u0[x + 2]
        m0, m1, m2, m3 = sums
        return (
            m0 + fold(start * start),
            m1 + fold(start * second),
            m2 + fold(second * second),
            m3 + fold(second * image),
        )

    lhs_p = jnp.concatenate(
        [jnp.concatenate([byt[0], byt[0]], axis=1), jnp.concatenate([byt[1], byt[1]], axis=1)], axis=0
    )
    fields = ((xe, 3), (u0, 2), (u1, 1))

    def put_proj(x):
        p = pe[x + 1]
        upper = jnp.where(jnp.logical_and(last, x == LX - 1), 1.0, 0.5)
        lower = jnp.where(jnp.logical_and(first, x == 0), 1.0, 0.5)
        p_rim = rim * p
        p_up = upper * (pe[x + 2] - p)
        p_down = lower * (p - pe[x])
        p_y = inner_y * (pltpu.roll(p, NG - 1, 0) - p)
        p_z = inner_z * (pltpu.roll(p, NG - 1, 1) - p)
        k = kp[x + HALO]
        parts = []
        for ref, at in fields:
            a = ref[x + at]
            total = p_rim * a + (ref[x + at + 1] - a) * p_up + (a - ref[x + at - 1]) * p_down
            qy = (pltpu.roll(a, NG - 1, 0) - a) * p_y
            total = total + (qy + pltpu.roll(qy, 1, 0))
            qz = (pltpu.roll(a, NG - 1, 1) - a) * p_z
            total = total + (qz + pltpu.roll(qz, 1, 1))
            parts.append(jnp.concatenate(pieces(k * total, 2), axis=0))
        got = mm(lhs_p, jnp.concatenate(parts, axis=1))
        got = got[:M] + got[M:]
        for f in range(3):
            pbuf[f, x] = got[:, f * NG : (f + 1) * NG]

    def mix_x(layers, fresh):
        def one(i, carry):
            for f in range(3):
                total = None if fresh else qbuf[f, i]
                for x in layers:
                    term = bx_ref[i, s * LX + x] * pbuf[f, x]
                    total = term if total is None else total + term
                qbuf[f, i] = total
            return carry

        lax.fori_loop(0, M, one, 0)

    def outer(t, count, width):
        return t + jnp.where(t >= width, count - 2 * width, 0)

    load_x.wait()
    lax.fori_loop(3, 17, lambda e, c: (put_u0(e), c)[1], 0)
    lax.fori_loop(3, 15, lambda e, c: (put_u1(e), c)[1], 0)
    zero = jnp.zeros((8, NG), F32)
    sums = lax.fori_loop(3, 13, moments, (zero, zero, zero, zero))
    lax.fori_loop(3, 13, lambda x, c: (put_proj(x), c)[1], 0)
    mix_x(range(3, 13), True)

    load_c.wait()
    pltpu.make_async_copy(cs.at[pl.ds(1, NP - 1)], cs.at[pl.ds(1, NP - 1)], c_recv).wait()
    every = cs[...]
    mine = cs[0]
    gap = every - mine[None]
    near = jnp.sum(jnp.sum(gap * gap, axis=1), axis=1, keepdims=True)
    center = jnp.sum(every, axis=0) * (1.0 / NP)
    off = every - center[None]
    spread = jnp.sum(jnp.sum(off * off, axis=0), keepdims=True) * (2.0 / (NP - 1))
    lane32 = lax.broadcasted_iota(jnp.int32, (NP, NG), 1)
    diag = lane32 == lax.broadcasted_iota(jnp.int32, (NP, NG), 0)
    near_row = jnp.sum(jnp.where(diag, near, 0.0), axis=0, keepdims=True)
    near_row = jnp.where(lane32[0:1] == NP, spread, near_row)
    tail = jnp.concatenate([jnp.broadcast_to(tau, (1, NG)), near_row, jnp.zeros((6, NG), F32)], axis=0)

    @pl.when(jnp.logical_not(first))
    def _():
        x_up().wait_recv()
        r_up().wait_recv()

    @pl.when(jnp.logical_not(last))
    def _():
        x_down().wait_recv()
        r_down().wait_recv()

    lax.fori_loop(0, 6, lambda t, c: (put_u0(outer(t, LX + 4, 3)), c)[1], 0)
    lax.fori_loop(0, 6, lambda t, c: (put_u1(outer(t, LX + 2, 3)), c)[1], 0)
    sums = lax.fori_loop(0, 6, lambda t, c: moments(outer(t, LX, 3), c), sums)

    @pl.when(jnp.logical_not(first))
    def _():
        p_up().wait_recv()

    @pl.when(jnp.logical_not(last))
    def _():
        p_down().wait_recv()

    lax.fori_loop(0, 6, lambda t, c: (put_proj(outer(t, LX, 3)), c)[1], 0)
    mix_x((0, 1, 2, 13, 14, 15), False)

    q_two = jnp.concatenate(pieces(qbuf[...].reshape(3 * M * M, NG), 2), axis=1)
    lhs_z = jnp.concatenate(
        [jnp.concatenate([bzt[0], bzt[0]], axis=1), jnp.concatenate([bzt[1], bzt[1]], axis=1)], axis=0
    )
    tensor = mm_nt(lhs_z, q_two)
    tensor = tensor[:M] + tensor[M:]
    parts = []
    for f in range(3):
        parts += pieces(tensor[:, f * M * M : (f + 1) * M * M], 2)
    rhs = jnp.concatenate(parts, axis=0)

    m3 = sums[3] * tau
    rows = [jnp.sum(m, axis=0, keepdims=True) for m in (sums[0], sums[1], sums[2], m3)]
    head = jnp.concatenate(rows, axis=0)

    def fill(ref, r):
        share = lax.rem(s + r, NS)
        cols = pl.ds(pl.multiple_of(share * SH, SH), SH)
        got = mm(rhs, hot[:, cols])
        low = lhot[:, cols]
        for f in range(3):
            at = 2 * M * f
            row = jnp.sum((got[at : at + M] + got[at + M : at + 2 * M]) * low, axis=0, keepdims=True)
            for q in range(SH // NG):
                ref[r, 4 * f + q : 4 * f + q + 1, :] = row[:, q * NG : (q + 1) * NG]
        ref[r, 12:16, :] = head
        ref[r, 16:24, :] = tail

    def share_send(r, carry):
        fill(pk, r)
        remote(pk.at[r], rp.at[NS - r], r_send, r_recv, peer_s(r)).start()
        return carry

    lax.fori_loop(1, NS, share_send, 0)
    fill(rp, 0)
    pltpu.make_async_copy(rp.at[pl.ds(1, NS - 1)], rp.at[pl.ds(1, NS - 1)], r_recv).wait()

    taus = rp[:, 16:17, :]
    least = jnp.min(taus, axis=0)
    ratio = least[None] / taus
    q0 = jnp.sum(jnp.sum(rp[:, 12:13, :], axis=0), axis=1, keepdims=True)
    q1 = jnp.sum(jnp.sum(rp[:, 13:14, :] * ratio, axis=0), axis=1, keepdims=True)
    q2 = jnp.sum(jnp.sum(rp[:, 14:15, :] * ratio * ratio, axis=0), axis=1, keepdims=True)
    q3 = jnp.sum(jnp.sum(rp[:, 15:16, :] * ratio * ratio * ratio, axis=0), axis=1, keepdims=True)
    proj0 = jnp.sum(rp[:, 0:4, :], axis=0)
    proj1 = jnp.sum(rp[:, 4:8, :], axis=0)
    proj2 = jnp.sum(rp[:, 8:12, :] * ratio, axis=0)
    alpha = q0 / q1
    norm = alpha * alpha * q2 - q0
    grown = norm / q0 + 1.0
    alpha1 = norm / (alpha * alpha * (q3 - q2 * (q2 / q1)))
    tau0 = least[:, 0:1]
    scale0 = tau0 * (alpha + alpha1 * grown)
    scale2 = -(tau0 * alpha1) * alpha
    gs[0] = proj0 + scale0 * proj1 + scale2 * proj2

    def send_g(r, carry):
        remote(gs.at[0], gs.at[NP - r], g_send, g_recv, peer_p(r)).start()
        return carry

    lax.fori_loop(1, NP, send_g, 0)

    scale1 = scale2 * (tau0 / tau)

    def put_x(x, carry):
        xo[x] = xe[x + 3] + scale0 * u0[x + 2] + scale1 * u1[x + 1]
        return carry

    lax.fori_loop(0, LX, put_x, 0)
    store = pltpu.make_async_copy(xo, adj_hbm, out_sem)
    store.start()

    near_all = jnp.sum(rp[:, 17:18, :], axis=0)
    width = near_all[:, NP : NP + 1]
    kern = jnp.exp(-near_all / width)
    kcol = jnp.sum(jnp.where(diag, kern, 0.0), axis=1, keepdims=True)
    weight = jnp.broadcast_to(kcol[:, :, None], (NP, 1, NG))
    drive = jnp.sum(weight * every, axis=0)
    repel = jnp.sum(weight * (mine[None] - every), axis=0)
    base = mine + (STEP / NP) * ((2.0 / width) * repel - drive)

    pltpu.make_async_copy(gs.at[pl.ds(1, NP - 1)], gs.at[pl.ds(1, NP - 1)], g_recv).wait()
    new_ref[...] = base - (STEP / NP) * jnp.sum(weight * gs[...], axis=0)

    def sent(ref, sem):
        pltpu.make_async_copy(ref, ref, sem).wait()

    sent(cs.at[pl.ds(1, NP - 1)], c_send)
    sent(rp.at[pl.ds(1, NS - 1)], r_send)
    sent(gs.at[pl.ds(1, NP - 1)], g_send)

    @pl.when(jnp.logical_not(last))
    def _():
        x_up().wait_send()
        p_up().wait_send()
        r_up().wait_send()

    @pl.when(jnp.logical_not(first))
    def _():
        x_down().wait_send()
        p_down().wait_send()
        r_down().wait_send()

    store.wait()


def shards(coeffs, modes, basis_x, basis_y, basis_z, pressure, initial_adjoint, sensors, observed, precision):
    vmem = pl.BlockSpec(memory_space=pltpu.VMEM)
    smem = pl.BlockSpec(memory_space=pltpu.SMEM)
    anywhere = pl.BlockSpec(memory_space=pl.ANY)
    dma = pltpu.SemaphoreType.DMA
    layers = lambda count: pltpu.VMEM((count, NG, NG), F32)
    new, adjoint = pl.pallas_call(
        kernel,
        out_shape=(
            jax.ShapeDtypeStruct((SH // NG, NG), F32),
            jax.ShapeDtypeStruct((LX, NG, NG), F32),
        ),
        in_specs=[anywhere, vmem, smem, vmem, vmem, anywhere, anywhere, smem, smem, smem],
        out_specs=(vmem, anywhere),
        scratch_shapes=[
            layers(LX + 6),
            layers(LX + 2),
            layers(LX + 6),
            layers(LX + 6),
            layers(LX + 6),
            layers(LX + 6),
            layers(LX + 6),
            layers(LX + 4),
            layers(LX + 2),
            layers(LX),
            pltpu.VMEM((LX + 4, 8, NG), F32),
            pltpu.VMEM((M * M, K), BF16),
            pltpu.VMEM((M, K), F32),
            pltpu.VMEM((3 * M, K), BF16),
            pltpu.VMEM((M, M, NG), F32),
            pltpu.VMEM((3, LX, M, NG), F32),
            pltpu.VMEM((3, M, M, NG), F32),
            pltpu.VMEM((NP, SH // NG, NG), F32),
            pltpu.VMEM((NS, SH // NG, NG), F32),
            pltpu.VMEM((NS, 24, NG), F32),
            pltpu.VMEM((NS, 24, NG), F32),
            pltpu.VMEM((NP, SH // NG, NG), F32),
            dma((3,)), dma, dma((6,)), dma((6,)),
            dma, dma, dma, dma, dma, dma, dma,
        ],
        compiler_params=pltpu.CompilerParams(
            collective_id=0, has_side_effects=True, vmem_limit_bytes=60 * 2**20
        ),
    )(
        coeffs.reshape(NS, SH // NG, NG),
        modes.reshape(K // NG, NG),
        basis_x.T,
        basis_y.T,
        basis_z.T,
        pressure[0],
        initial_adjoint[0],
        sensors,
        observed,
        precision,
    )
    return new.reshape(1, SH), adjoint[None]


def solution(mesh):
    in_specs = (
        P("particle", None),
        P(),
        P(),
        P(),
        P(),
        P("particle", "space", None, None),
        P("particle", "space", None, None),
        P(),
        P(),
        P(),
    )
    out_specs = (P("particle", "space"), P("particle", "space", None, None))
    return jax.shard_map(shards, mesh=mesh, in_specs=in_specs, out_specs=out_specs, check_vma=False)
```

```python
import jax
import jax.numpy as jnp
from jax import lax
from jax.experimental import pallas as pl
from jax.experimental.pallas import tpu as pltpu
from jax.sharding import PartitionSpec as P

F32 = jnp.float32
BF16 = jnp.bfloat16
NP = 32
NS = 8
LX = 16
NX = 128
NG = 128
M = 16
K = M * M * M
SH = K // NS
HALO = 3
STEP = 0.5
NN = (((1,), (1,)), ((), ()))


def pieces(value, count):
    out = []
    rest = value
    for _ in range(count):
        part = rest.astype(BF16)
        out.append(part)
        rest = rest - part.astype(F32)
    return out


def mm(a, b):
    return jnp.dot(a, b, preferred_element_type=F32)


def mm_nt(a, b):
    return lax.dot_general(a, b, NN, preferred_element_type=F32)


def fold(value):
    return jnp.sum(value.reshape(NG // 8, 8, NG), axis=0)


def kernel(
    c_hbm, modes_ref, bx_ref, by_ref, bz_ref, p_hbm, x_hbm, sens_ref, obs_ref, prec_ref,
    new_ref, adj_ref,
    xe, pe, kp, kx, ky, kz, kb, wf, u0, u1, rsum, hot, lhot, lcs, fbuf, pbuf, qbuf,
    cs, wk, pk, rp, gs,
    in_sem, halo_send, halo_recv, c_own, c_send, c_recv, r_send, r_recv, g_send, g_recv,
):
    n = lax.axis_index("particle")
    s = lax.axis_index("space")
    first = s == 0
    last = s == NS - 1

    def far(j, count):
        half = (j + 1) // 2
        return count // 2 + jnp.where(lax.rem(j, 2) == 0, -half, half)

    def peer_p(r):
        return {"particle": lax.rem(n + r, NP)}

    def peer_s(r):
        return {"space": lax.rem(s + r, NS)}

    barrier = pltpu.get_barrier_semaphore()

    def greet_s(r, carry):
        pl.semaphore_signal(barrier, inc=1, device_id=peer_s(r))
        return carry

    def greet_p(j, carry):
        pl.semaphore_signal(barrier, inc=1, device_id=peer_p(far(j, NP)))
        return carry

    lax.fori_loop(0, NP - 1, greet_p, 0)
    lax.fori_loop(1, NS, greet_s, 0)

    load_x = pltpu.make_async_copy(x_hbm, xe.at[pl.ds(HALO, LX)], in_sem.at[0])
    load_p = pltpu.make_async_copy(p_hbm, pe.at[pl.ds(1, LX)], in_sem.at[1])
    load_c = pltpu.make_async_copy(c_hbm.at[s], cs.at[0], c_own)
    load_all = pltpu.make_async_copy(c_hbm, wk, in_sem.at[2])
    load_all.start()
    load_p.start()
    load_x.start()
    load_c.start()

    load_all.wait()
    row_id = lax.broadcasted_iota(jnp.int32, (M * M, NG), 0)
    sub_id = lax.broadcasted_iota(jnp.int32, (M, NG), 0)
    for chunk in range(K // NG):
        pos = modes_ref[chunk : chunk + 1, :]
        cols = slice(chunk * NG, (chunk + 1) * NG)
        upper = lax.shift_right_logical(pos, 4)
        lower = lax.bitwise_and(pos, 15)
        hot[:, cols] = jnp.where(row_id == upper, 1.0, 0.0).astype(BF16)
        low = jnp.where(sub_id == lower, 1.0, 0.0)
        lhot[:, cols] = low
        own = wk[chunk // 4, chunk % 4 : chunk % 4 + 1, :]
        for q, part in enumerate(pieces(own, 3)):
            lcs[q * M : (q + 1) * M, cols] = (low * part.astype(F32)).astype(BF16)

    lane = lax.broadcasted_iota(jnp.int32, (NG, NG), 1)
    suby = lax.broadcasted_iota(jnp.int32, (NG, NG), 0)
    eye = jnp.where(lane == suby, 1.0, 0.0).astype(BF16)
    byt = pieces(by_ref[...], 3)
    bzt = pieces(bz_ref[...], 3)
    lhs_y = mm_nt(eye, jnp.concatenate([byt[which] for which in (0, 0, 1, 0, 1, 2)], axis=0)).astype(BF16)

    xi = mm_nt(hot[...], lcs[...]).astype(BF16)
    field = mm(xi, jnp.concatenate([bzt[0]] * 3, axis=0))
    field = field + mm(xi, jnp.concatenate([bzt[1]] * 3, axis=0))
    field = field + mm(xi, jnp.concatenate([bzt[2]] * 3, axis=0))
    fbuf[...] = field.reshape(M, M, NG)

    inner_y = jnp.where(suby == NG - 1, 0.0, 0.5)
    inner_z = jnp.where(lane == NG - 1, 0.0, 0.5)
    inner_ym = jnp.where(suby == 0, 0.0, 0.5)
    inner_zm = jnp.where(lane == 0, 0.0, 0.5)
    rim = (
        jnp.where(suby == NG - 1, 1.0, 0.0)
        + jnp.where(suby == 0, 1.0, 0.0)
        + jnp.where(lane == NG - 1, 1.0, 0.0)
        + jnp.where(lane == 0, 1.0, 0.0)
    )

    def mix(e):
        g = jnp.clip(s * LX - HALO + e, 0, NX - 1)
        total = bx_ref[0, g] * fbuf[0]
        for i in range(1, M):
            total = total + bx_ref[i, g] * fbuf[i]
        a, b, c = pieces(total, 3)
        return jnp.concatenate([a, b, a, c, b, a], axis=0)

    def faces(e, k, before):
        kp[e] = k
        ky[0, e] = inner_y * (k + pltpu.roll(k, NG - 1, 0))
        kz[0, e] = inner_z * (k + pltpu.roll(k, NG - 1, 1))
        ky[1, e] = inner_ym * (k + pltpu.roll(k, 1, 0))
        kz[1, e] = inner_zm * (k + pltpu.roll(k, 1, 1))
        kb[e] = rim * k
        kx[before] = 0.5 * (kp[before] + k)

    def log_layers(t, top):
        e = 2 * t
        both = jnp.exp(mm(lhs_y, jnp.concatenate([mix(e), mix(e + 1)], axis=1)))
        k0, k1 = both[:, :NG], both[:, NG:]
        faces(e, k0, max(e - 1, 0))
        faces(e + 1, k1, e)
        return jnp.maximum(top, jnp.max(jnp.maximum(k0, k1).reshape(NG // 8, 8, NG), axis=0))

    top = jnp.zeros((8, NG), F32)
    for t in range(HALO + LX // 2):
        top = log_layers(t, top)
    tau = (1.0 / 16.0) / jnp.max(top, keepdims=True)

    @pl.when(first)
    def _():
        xe[0:HALO] = jnp.zeros((HALO, NG, NG), F32)
        pe[0:1] = jnp.zeros((1, NG, NG), F32)
        rsum[0:2] = jnp.zeros((2, 8, NG), F32)

    @pl.when(last)
    def _():
        xe[HALO + LX :] = jnp.zeros((HALO, NG, NG), F32)
        pe[LX + 1 :] = jnp.zeros((1, NG, NG), F32)
        rsum[LX + 2 :] = jnp.zeros((2, 8, NG), F32)

    flat = (
        lax.broadcasted_iota(jnp.int32, (M, NG), 0) * NG + lax.broadcasted_iota(jnp.int32, (M, NG), 1)
    )

    def sensor_of(layer, block):
        index = layer * 8 + block
        return index, sens_ref[index] - index * (M * NG)

    load_p.wait()

    def misfit(x, carry):
        for b in range(8):
            index, cell = sensor_of(s * LX + x, b)
            part = pe[x + 1, b * M : (b + 1) * M, :]
            hit = jnp.where(flat == cell, (part - obs_ref[index]) * prec_ref[index], 0.0)
            rsum[x + 2, b : b + 1, :] = jnp.sum(hit, axis=0, keepdims=True)
        return carry

    lax.fori_loop(0, LX, misfit, 0)

    pl.semaphore_wait(barrier, NS - 1 + NP - 1)

    up = {"space": jnp.minimum(s + 1, NS - 1)}
    down = {"space": jnp.maximum(s - 1, 0)}

    def remote(src, dst, send, recv, where):
        return pltpu.make_async_remote_copy(src_ref=src, dst_ref=dst, send_sem=send, recv_sem=recv, device_id=where)

    def x_up():
        return remote(x_hbm.at[pl.ds(LX - HALO, HALO)], xe.at[pl.ds(0, HALO)], halo_send.at[0], halo_recv.at[0], up)

    def x_down():
        return remote(x_hbm.at[pl.ds(0, HALO)], xe.at[pl.ds(HALO + LX, HALO)], halo_send.at[1], halo_recv.at[1], down)

    def p_up():
        return remote(p_hbm.at[pl.ds(LX - 1, 1)], pe.at[pl.ds(0, 1)], halo_send.at[2], halo_recv.at[2], up)

    def p_down():
        return remote(p_hbm.at[pl.ds(0, 1)], pe.at[pl.ds(LX + 1, 1)], halo_send.at[3], halo_recv.at[3], down)

    def r_up():
        return remote(rsum.at[pl.ds(LX, 2)], rsum.at[pl.ds(0, 2)], halo_send.at[4], halo_recv.at[4], up)

    def r_down():
        return remote(rsum.at[pl.ds(2, 2)], rsum.at[pl.ds(LX + 2, 2)], halo_send.at[5], halo_recv.at[5], down)

    @pl.when(jnp.logical_not(last))
    def _():
        x_up().start()

    @pl.when(jnp.logical_not(first))
    def _():
        x_down().start()

    @pl.when(jnp.logical_not(last))
    def _():
        p_up().start()

    @pl.when(jnp.logical_not(first))
    def _():
        p_down().start()

    def send_c(r, carry):
        remote(c_hbm.at[s], cs.at[NP - r], c_send, c_recv, peer_p(r)).start()
        return carry

    @pl.when(jnp.logical_not(last))
    def _():
        r_up().start()

    @pl.when(jnp.logical_not(first))
    def _():
        r_down().start()

    lax.fori_loop(1, NP, send_c, 0)

    def differences(v_ref, i):
        v = v_ref[i]
        return (
            v - v_ref[i + 1],
            v - v_ref[i - 1],
            v - pltpu.roll(v, NG - 1, 0),
            v - pltpu.roll(v, 1, 0),
            v - pltpu.roll(v, NG - 1, 1),
            v - pltpu.roll(v, 1, 1),
            v,
        )

    def weigh(weights, parts):
        total = weights[0] * parts[0]
        for weight, part in zip(weights[1:], parts[1:]):
            total = total + weight * part
        return total

    def operator(d, e):
        return weigh((kx[e], kx[e - 1], ky[0, e], ky[1, e], kz[0, e], kz[1, e], kb[e]), d)

    def put_weights(x):
        k = kp[x + HALO]
        p = pe[x + 1]
        upper = jnp.where(jnp.logical_and(last, x == LX - 1), 1.0, 0.5)
        lower = jnp.where(jnp.logical_and(first, x == 0), 1.0, 0.5)
        wf[0, x] = (upper * k) * (p - pe[x + 2])
        wf[1, x] = (lower * k) * (p - pe[x])
        wf[2, x] = (inner_y * k) * (p - pltpu.roll(p, NG - 1, 0))
        wf[3, x] = (inner_ym * k) * (p - pltpu.roll(p, 1, 0))
        wf[4, x] = (inner_z * k) * (p - pltpu.roll(p, NG - 1, 1))
        wf[5, x] = (inner_zm * k) * (p - pltpu.roll(p, 1, 1))
        wf[6, x] = kb[x + HALO] * p

    lhs_p = jnp.concatenate(
        [jnp.concatenate([byt[0], byt[0]], axis=1), jnp.concatenate([byt[1], byt[1]], axis=1)], axis=0
    )

    def put_proj(f, layers, ds):
        parts = []
        for x, d in zip(layers, ds):
            grad = weigh(tuple(wf[j, x] for j in range(7)), d)
            parts.append(jnp.concatenate(pieces(grad, 2), axis=0))
        got = mm(lhs_p, jnp.concatenate(parts, axis=1))
        got = got[:M] + got[M:]
        for j, x in enumerate(layers):
            pbuf[f, x] = got[:, j * NG : (j + 1) * NG]

    def put_u0(x, d):
        g = s * LX + x
        safe = jnp.clip(g, 0, NX - 1)
        load = []
        for b in range(8):
            _, cell = sensor_of(safe, b)
            load.append(jnp.where(flat == cell, rsum[x + 2, b : b + 1, :], 0.0))
        u0[x + 2] = jnp.concatenate(load, axis=0) - operator(d, x + HALO)

    def put_u1(x, d):
        u1[x + 1] = operator(d, x + HALO) * tau

    def step_x(layers, project):
        ds = [differences(xe, x + 3) for x in layers]
        for x, d in zip(layers, ds):
            put_u0(x, d)
        if project:
            put_proj(0, layers, ds)

    def step_u0(layers, project):
        ds = [differences(u0, x + 2) for x in layers]
        for x, d in zip(layers, ds):
            put_u1(x, d)
        if project:
            put_proj(1, layers, ds)

    def step_u1(layers, sums):
        ds = [differences(u1, x + 1) for x in layers]
        m0, m1, m2, m3 = sums
        for x, d in zip(layers, ds):
            second, image = d[6], operator(d, x + HALO)
            start = u0[x + 2]
            m0 = m0 + fold(start * start)
            m1 = m1 + fold(start * second)
            m2 = m2 + fold(second * second)
            m3 = m3 + fold(second * image)
        put_proj(2, layers, ds)
        return m0, m1, m2, m3

    def mix_x(layers, fresh):
        def some(j, carry):
            for f in range(3):
                kept = [pbuf[f, x] for x in layers]
                for i in (4 * j, 4 * j + 1, 4 * j + 2, 4 * j + 3):
                    total = None if fresh else qbuf[f, i]
                    for x, part in zip(layers, kept):
                        term = bx_ref[i, s * LX + x] * part
                        total = term if total is None else total + term
                    qbuf[f, i] = total
            return carry

        lax.fori_loop(0, M // 4, some, 0)

    def pairs(lo, hi, step):
        def body(j, carry):
            step((lo + 2 * j, lo + 2 * j + 1))
            return carry

        lax.fori_loop(0, (hi - lo) // 2, body, 0)

    def around(j):
        return j, LX - 1 - j

    load_x.wait()
    pairs(1, LX - 1, lambda layers: [put_weights(x) for x in layers])
    pairs(1, LX - 1, lambda layers: step_x(layers, True))
    pairs(2, LX - 2, lambda layers: step_u0(layers, True))
    zero = jnp.zeros((8, NG), F32)
    sums = lax.fori_loop(
        0, LX // 2 - 3, lambda j, c: step_u1((3 + 2 * j, 4 + 2 * j), c), (zero, zero, zero, zero)
    )
    mix_x(range(3, 13), True)

    load_c.wait()
    pltpu.make_async_copy(cs.at[pl.ds(1, NP - 1)], cs.at[pl.ds(1, NP - 1)], c_recv).wait()
    every = cs[...]
    mine = cs[0]
    gap = every - mine[None]
    near = jnp.sum(jnp.sum(gap * gap, axis=1), axis=1, keepdims=True)
    center = jnp.sum(every, axis=0) * (1.0 / NP)
    off = every - center[None]
    spread = jnp.sum(jnp.sum(off * off, axis=0), keepdims=True) * (2.0 / (NP - 1))
    lane32 = lax.broadcasted_iota(jnp.int32, (NP, NG), 1)
    diag = lane32 == lax.broadcasted_iota(jnp.int32, (NP, NG), 0)
    near_row = jnp.sum(jnp.where(diag, near, 0.0), axis=0, keepdims=True)
    near_row = jnp.where(lane32[0:1] == NP, spread, near_row)
    tail = jnp.concatenate([jnp.broadcast_to(tau, (1, NG)), near_row, jnp.zeros((6, NG), F32)], axis=0)

    @pl.when(jnp.logical_not(first))
    def _():
        x_up().wait_recv()
        r_up().wait_recv()

    @pl.when(jnp.logical_not(last))
    def _():
        x_down().wait_recv()
        r_down().wait_recv()

    @pl.when(jnp.logical_not(first))
    def _():
        p_up().wait_recv()

    @pl.when(jnp.logical_not(last))
    def _():
        p_down().wait_recv()

    for x in around(0):
        put_weights(x)
    step_x(around(-2), False)
    step_x(around(-1), False)
    step_x(around(0), True)

    @pl.when(first)
    def _():
        u0[0:2] = jnp.zeros((2, NG, NG), F32)

    @pl.when(last)
    def _():
        u0[LX + 2 :] = jnp.zeros((2, NG, NG), F32)

    step_u0(around(-1), False)
    step_u0(around(0), True)
    step_u0(around(1), True)

    @pl.when(first)
    def _():
        u1[0:1] = jnp.zeros((1, NG, NG), F32)

    @pl.when(last)
    def _():
        u1[LX + 1 :] = jnp.zeros((1, NG, NG), F32)

    for j in range(3):
        sums = step_u1(around(j), sums)
    mix_x((0, 1, 2, 13, 14, 15), False)

    q_two = jnp.concatenate(pieces(qbuf[...].reshape(3 * M * M, NG), 2), axis=1)
    lhs_z = jnp.concatenate(
        [jnp.concatenate([bzt[0], bzt[0]], axis=1), jnp.concatenate([bzt[1], bzt[1]], axis=1)], axis=0
    )
    tensor = mm_nt(lhs_z, q_two)
    tensor = tensor[:M] + tensor[M:]
    parts = []
    for f in range(3):
        parts += pieces(tensor[:, f * M * M : (f + 1) * M * M], 2)
    rhs = jnp.concatenate(parts, axis=0)

    m3 = sums[3] * tau
    rows = [
        jnp.broadcast_to(jnp.sum(jnp.sum(m, axis=0, keepdims=True), axis=1, keepdims=True), (1, NG))
        for m in (sums[0], sums[1], sums[2], m3)
    ]
    head = jnp.concatenate(rows, axis=0)

    for share in range(NS):
        cols = slice(share * SH, (share + 1) * SH)
        got = mm(rhs, hot[:, cols])
        low = lhot[:, cols]
        for f in range(3):
            at = 2 * M * f
            row = jnp.sum((got[at : at + M] + got[at + M : at + 2 * M]) * low, axis=0, keepdims=True)
            for q in range(SH // NG):
                pk[share, 4 * f + q : 4 * f + q + 1, :] = row[:, q * NG : (q + 1) * NG]
        pk[share, 12:16, :] = head
        pk[share, 16:24, :] = tail

    def share_send(j, carry):
        r = far(j, NS)
        remote(pk.at[lax.rem(s + r, NS)], rp.at[NS - r], r_send, r_recv, peer_s(r)).start()
        return carry

    lax.fori_loop(0, NS - 1, share_send, 0)
    rp[0] = pk[s]
    pltpu.make_async_copy(rp.at[pl.ds(1, NS - 1)], rp.at[pl.ds(1, NS - 1)], r_recv).wait()

    taus = rp[:, 16:17, :]
    least = jnp.min(taus, axis=0)
    ratio = least[None] / taus
    q0 = jnp.sum(rp[:, 12:13, :], axis=0)
    q1 = jnp.sum(rp[:, 13:14, :] * ratio, axis=0)
    q2 = jnp.sum(rp[:, 14:15, :] * (ratio * ratio), axis=0)
    q3 = jnp.sum(rp[:, 15:16, :] * (ratio * ratio * ratio), axis=0)
    proj0 = jnp.sum(rp[:, 0:4, :], axis=0)
    proj1 = jnp.sum(rp[:, 4:8, :], axis=0)
    proj2 = jnp.sum(rp[:, 8:12, :] * ratio, axis=0)
    alpha = q0 / q1
    norm = alpha * alpha * q2 - q0
    grown = norm / q0 + 1.0
    alpha1 = norm / (alpha * alpha * (q3 - q2 * (q2 / q1)))
    tau0 = least
    scale0 = tau0 * (alpha + alpha1 * grown)
    scale2 = -(tau0 * alpha1) * alpha
    gs[0] = proj0 + scale0 * proj1 + scale2 * proj2

    def send_g(j, carry):
        r = far(j, NP)
        remote(gs.at[0], gs.at[NP - r], g_send, g_recv, peer_p(r)).start()
        return carry

    lax.fori_loop(0, NP - 1, send_g, 0)

    scale1 = scale2 * (tau0 / tau)

    def put_x(x, carry):
        adj_ref[x] = xe[x + 3] + scale0 * u0[x + 2] + scale1 * u1[x + 1]
        return carry

    lax.fori_loop(0, LX, put_x, 0)

    near_all = jnp.sum(rp[:, 17:18, :], axis=0)
    width = near_all[:, NP : NP + 1]
    kern = jnp.exp(-near_all / width)
    kcol = jnp.sum(jnp.where(diag, kern, 0.0), axis=1, keepdims=True)
    weight = jnp.broadcast_to(kcol[:, :, None], (NP, 1, NG))
    drive = jnp.sum(weight * every, axis=0)
    repel = jnp.sum(weight * (mine[None] - every), axis=0)
    base = mine + (STEP / NP) * ((2.0 / width) * repel - drive)

    pltpu.make_async_copy(gs.at[pl.ds(1, NP - 1)], gs.at[pl.ds(1, NP - 1)], g_recv).wait()
    new_ref[...] = base - (STEP / NP) * jnp.sum(weight * gs[...], axis=0)

    def sent(ref, sem):
        pltpu.make_async_copy(ref, ref, sem).wait()

    sent(cs.at[pl.ds(1, NP - 1)], c_send)
    sent(rp.at[pl.ds(1, NS - 1)], r_send)
    sent(gs.at[pl.ds(1, NP - 1)], g_send)

    @pl.when(jnp.logical_not(last))
    def _():
        x_up().wait_send()
        p_up().wait_send()
        r_up().wait_send()

    @pl.when(jnp.logical_not(first))
    def _():
        x_down().wait_send()
        p_down().wait_send()
        r_down().wait_send()


def shards(coeffs, modes, basis_x, basis_y, basis_z, pressure, initial_adjoint, sensors, observed, precision):
    vmem = pl.BlockSpec(memory_space=pltpu.VMEM)
    smem = pl.BlockSpec(memory_space=pltpu.SMEM)
    hbm = pl.BlockSpec(memory_space=pltpu.HBM)
    dma = pltpu.SemaphoreType.DMA
    layers = lambda count: pltpu.VMEM((count, NG, NG), F32)
    new, adjoint = pl.pallas_call(
        kernel,
        out_shape=(
            pltpu.VMEM((SH // NG, NG), F32),
            pltpu.VMEM((LX, NG, NG), F32),
        ),
        in_specs=[hbm, vmem, smem, vmem, vmem, hbm, hbm, smem, smem, smem],
        out_specs=(vmem, vmem),
        scratch_shapes=[
            layers(LX + 6),
            layers(LX + 2),
            layers(LX + 6),
            layers(LX + 6),
            pltpu.VMEM((2, LX + 6, NG, NG), F32),
            pltpu.VMEM((2, LX + 6, NG, NG), F32),
            layers(LX + 6),
            pltpu.VMEM((7, LX, NG, NG), F32),
            layers(LX + 4),
            layers(LX + 2),
            pltpu.VMEM((LX + 4, 8, NG), F32),
            pltpu.VMEM((M * M, K), BF16),
            pltpu.VMEM((M, K), F32),
            pltpu.VMEM((3 * M, K), BF16),
            pltpu.VMEM((M, M, NG), F32),
            pltpu.VMEM((3, LX, M, NG), F32),
            pltpu.VMEM((3, M, M, NG), F32),
            pltpu.VMEM((NP, SH // NG, NG), F32),
            pltpu.VMEM((NS, SH // NG, NG), F32),
            pltpu.VMEM((NS, 24, NG), F32),
            pltpu.VMEM((NS, 24, NG), F32),
            pltpu.VMEM((NP, SH // NG, NG), F32),
            dma((3,)), dma((6,)), dma((6,)),
            dma, dma, dma, dma, dma, dma, dma,
        ],
        compiler_params=pltpu.CompilerParams(
            collective_id=0, has_side_effects=True, vmem_limit_bytes=60 * 2**20
        ),
    )(
        coeffs.reshape(NS, SH // NG, NG),
        modes.reshape(K // NG, NG),
        basis_x.T,
        basis_y.T,
        basis_z.T,
        pressure[0],
        initial_adjoint[0],
        sensors,
        observed,
        precision,
    )
    return new.reshape(1, SH), adjoint[None]


def solution(mesh):
    in_specs = (
        P("particle", None),
        P(),
        P(),
        P(),
        P(),
        P("particle", "space", None, None),
        P("particle", "space", None, None),
        P(),
        P(),
        P(),
    )
    out_specs = (P("particle", "space"), P("particle", "space", None, None))
    return jax.shard_map(shards, mesh=mesh, in_specs=in_specs, out_specs=out_specs, check_vma=False)
```

```python
import jax
import jax.numpy as jnp
from jax import lax
from jax.experimental import pallas as pl
from jax.experimental.pallas import tpu as pltpu
from jax.sharding import PartitionSpec as P

F32 = jnp.float32
BF16 = jnp.bfloat16
NP = 32
NS = 8
LX = 16
NX = 128
NG = 128
M = 16
K = M * M * M
SH = K // NS
HALO = 3
STEP = 0.5
NN = (((1,), (1,)), ((), ()))


def pieces(value, count):
    out = []
    rest = value
    for _ in range(count):
        part = rest.astype(BF16)
        out.append(part)
        rest = rest - part.astype(F32)
    return out


def mm(a, b):
    return jnp.dot(a, b, preferred_element_type=F32)


def mm_nt(a, b):
    return lax.dot_general(a, b, NN, preferred_element_type=F32)


def fold(value):
    return jnp.sum(value.reshape(NG // 8, 8, NG), axis=0)


def kernel(
    c_hbm, modes_in, bx_in, by_in, bz_in, p_hbm, x_hbm, sens_in, obs_in, prec_in,
    new_ref, adj_ref,
    modes_ref, bx_ref, by_ref, bz_ref, sens_ref, obs_ref, prec_ref, xe, pe, kp, kx, ky, kz, kb, wf, u0, u1, rsum, hot, lhot, lcs, fbuf, pbuf, qbuf,
    cs, wk, pk, rp, gs,
    in_sem, small_sem, halo_send, halo_recv, c_own, c_send, c_recv, r_send, r_recv, g_send, g_recv,
):
    n = lax.axis_index("particle")
    s = lax.axis_index("space")
    first = s == 0
    last = s == NS - 1

    def far(j, count):
        half = (j + 1) // 2
        return count // 2 + (half if j % 2 else -half)

    def peer_p(r):
        return {"particle": lax.rem(n + r, NP)}

    def peer_s(r):
        return {"space": lax.rem(s + r, NS)}

    barrier = pltpu.get_barrier_semaphore()

    load_x = pltpu.make_async_copy(x_hbm, xe.at[pl.ds(HALO, LX)], in_sem.at[0])
    load_p = pltpu.make_async_copy(p_hbm, pe.at[pl.ds(1, LX)], in_sem.at[1])
    load_c = pltpu.make_async_copy(c_hbm.at[s], cs.at[0], c_own)
    load_all = pltpu.make_async_copy(c_hbm, wk, in_sem.at[2])
    small = (
        (modes_in, modes_ref), (bx_in, bx_ref), (by_in, by_ref), (bz_in, bz_ref),
        (sens_in, sens_ref), (obs_in, obs_ref), (prec_in, prec_ref),
    )
    load_small = [pltpu.make_async_copy(src, dst, small_sem.at[j]) for j, (src, dst) in enumerate(small)]
    load_all.start()
    load_small[0].start()

    for j in range(NP - 1):
        pl.semaphore_signal(barrier, inc=1, device_id=peer_p(far(j, NP)))
    for r in range(1, NS):
        pl.semaphore_signal(barrier, inc=1, device_id=peer_s(r))

    for load in load_small[1:]:
        load.start()
    load_p.start()
    load_x.start()
    load_c.start()

    load_all.wait()
    load_small[0].wait()
    row_id = lax.broadcasted_iota(jnp.int32, (M * M, NG), 0)
    sub_id = lax.broadcasted_iota(jnp.int32, (M, NG), 0)
    for chunk in range(K // NG):
        pos = modes_ref[chunk : chunk + 1, :]
        cols = slice(chunk * NG, (chunk + 1) * NG)
        upper = lax.shift_right_logical(pos, 4)
        lower = lax.bitwise_and(pos, 15)
        hot[:, cols] = jnp.where(row_id == upper, 1.0, 0.0).astype(BF16)
        low = jnp.where(sub_id == lower, 1.0, 0.0)
        lhot[:, cols] = low
        own = wk[chunk // 4, chunk % 4 : chunk % 4 + 1, :]
        for q, part in enumerate(pieces(own, 3)):
            lcs[q * M : (q + 1) * M, cols] = (low * part.astype(F32)).astype(BF16)

    lane = lax.broadcasted_iota(jnp.int32, (NG, NG), 1)
    suby = lax.broadcasted_iota(jnp.int32, (NG, NG), 0)
    eye = jnp.where(lane == suby, 1.0, 0.0).astype(BF16)
    for load in load_small[1:4]:
        load.wait()
    byt = pieces(by_ref[...], 3)
    bzt = pieces(bz_ref[...], 3)
    lhs_y = mm_nt(eye, jnp.concatenate([byt[which] for which in (0, 0, 1, 0, 1, 2)], axis=0)).astype(BF16)

    xi = mm_nt(hot[...], lcs[...]).astype(BF16)
    field = mm(xi, jnp.concatenate([bzt[0]] * 3, axis=0))
    field = field + mm(xi, jnp.concatenate([bzt[1]] * 3, axis=0))
    field = field + mm(xi, jnp.concatenate([bzt[2]] * 3, axis=0))
    fbuf[...] = field.reshape(M, M, NG)

    inner_y = jnp.where(suby == NG - 1, 0.0, 0.5)
    inner_z = jnp.where(lane == NG - 1, 0.0, 0.5)
    inner_ym = jnp.where(suby == 0, 0.0, 0.5)
    inner_zm = jnp.where(lane == 0, 0.0, 0.5)
    rim = (
        jnp.where(suby == NG - 1, 1.0, 0.0)
        + jnp.where(suby == 0, 1.0, 0.0)
        + jnp.where(lane == NG - 1, 1.0, 0.0)
        + jnp.where(lane == 0, 1.0, 0.0)
    )

    def mix(e):
        g = jnp.clip(s * LX - HALO + e, 0, NX - 1)
        total = bx_ref[0, g] * fbuf[0]
        for i in range(1, M):
            total = total + bx_ref[i, g] * fbuf[i]
        a, b, c = pieces(total, 3)
        return jnp.concatenate([a, b, a, c, b, a], axis=0)

    def faces(e, k, before):
        kp[e] = k
        ky[0, e] = inner_y * (k + pltpu.roll(k, NG - 1, 0))
        kz[0, e] = inner_z * (k + pltpu.roll(k, NG - 1, 1))
        ky[1, e] = inner_ym * (k + pltpu.roll(k, 1, 0))
        kz[1, e] = inner_zm * (k + pltpu.roll(k, 1, 1))
        kb[e] = rim * k
        kx[before] = 0.5 * (kp[before] + k)

    def log_layers(t, top):
        e = 2 * t
        both = jnp.exp(mm(lhs_y, jnp.concatenate([mix(e), mix(e + 1)], axis=1)))
        k0, k1 = both[:, :NG], both[:, NG:]
        faces(e, k0, max(e - 1, 0))
        faces(e + 1, k1, e)
        return jnp.maximum(top, jnp.max(jnp.maximum(k0, k1).reshape(NG // 8, 8, NG), axis=0))

    top = jnp.zeros((8, NG), F32)
    for t in range(HALO + LX // 2):
        top = log_layers(t, top)
    tau = (1.0 / 16.0) / jnp.max(top, keepdims=True)

    @pl.when(first)
    def _():
        xe[0:HALO] = jnp.zeros((HALO, NG, NG), F32)
        pe[0:1] = jnp.zeros((1, NG, NG), F32)
        rsum[0:2] = jnp.zeros((2, 8, NG), F32)

    @pl.when(last)
    def _():
        xe[HALO + LX :] = jnp.zeros((HALO, NG, NG), F32)
        pe[LX + 1 :] = jnp.zeros((1, NG, NG), F32)
        rsum[LX + 2 :] = jnp.zeros((2, 8, NG), F32)

    flat = (
        lax.broadcasted_iota(jnp.int32, (M, NG), 0) * NG + lax.broadcasted_iota(jnp.int32, (M, NG), 1)
    )

    def sensor_of(layer, block):
        index = layer * 8 + block
        return index, sens_ref[index] - index * (M * NG)

    load_p.wait()
    for load in load_small[4:]:
        load.wait()

    def misfit(x, carry):
        for b in range(8):
            index, cell = sensor_of(s * LX + x, b)
            part = pe[x + 1, b * M : (b + 1) * M, :]
            hit = jnp.where(flat == cell, (part - obs_ref[index]) * prec_ref[index], 0.0)
            rsum[x + 2, b : b + 1, :] = jnp.sum(hit, axis=0, keepdims=True)
        return carry

    lax.fori_loop(0, LX, misfit, 0)

    pl.semaphore_wait(barrier, NS - 1 + NP - 1)

    up = {"space": jnp.minimum(s + 1, NS - 1)}
    down = {"space": jnp.maximum(s - 1, 0)}

    def remote(src, dst, send, recv, where):
        return pltpu.make_async_remote_copy(src_ref=src, dst_ref=dst, send_sem=send, recv_sem=recv, device_id=where)

    def x_up():
        return remote(x_hbm.at[pl.ds(LX - HALO, HALO)], xe.at[pl.ds(0, HALO)], halo_send.at[0], halo_recv.at[0], up)

    def x_down():
        return remote(x_hbm.at[pl.ds(0, HALO)], xe.at[pl.ds(HALO + LX, HALO)], halo_send.at[1], halo_recv.at[1], down)

    def p_up():
        return remote(p_hbm.at[pl.ds(LX - 1, 1)], pe.at[pl.ds(0, 1)], halo_send.at[2], halo_recv.at[2], up)

    def p_down():
        return remote(p_hbm.at[pl.ds(0, 1)], pe.at[pl.ds(LX + 1, 1)], halo_send.at[3], halo_recv.at[3], down)

    def r_up():
        return remote(rsum.at[pl.ds(LX, 2)], rsum.at[pl.ds(0, 2)], halo_send.at[4], halo_recv.at[4], up)

    def r_down():
        return remote(rsum.at[pl.ds(2, 2)], rsum.at[pl.ds(LX + 2, 2)], halo_send.at[5], halo_recv.at[5], down)

    @pl.when(jnp.logical_not(last))
    def _():
        x_up().start()

    @pl.when(jnp.logical_not(first))
    def _():
        x_down().start()

    @pl.when(jnp.logical_not(last))
    def _():
        p_up().start()

    @pl.when(jnp.logical_not(first))
    def _():
        p_down().start()

    def send_c(r, carry):
        remote(c_hbm.at[s], cs.at[NP - r], c_send, c_recv, peer_p(r)).start()
        return carry

    @pl.when(jnp.logical_not(last))
    def _():
        r_up().start()

    @pl.when(jnp.logical_not(first))
    def _():
        r_down().start()

    lax.fori_loop(1, NP, send_c, 0)

    def differences(v_ref, i):
        v = v_ref[i]
        return (
            v - v_ref[i + 1],
            v - v_ref[i - 1],
            v - pltpu.roll(v, NG - 1, 0),
            v - pltpu.roll(v, 1, 0),
            v - pltpu.roll(v, NG - 1, 1),
            v - pltpu.roll(v, 1, 1),
            v,
        )

    def weigh(weights, parts):
        total = weights[0] * parts[0]
        for weight, part in zip(weights[1:], parts[1:]):
            total = total + weight * part
        return total

    def operator(d, e):
        return weigh((kx[e], kx[e - 1], ky[0, e], ky[1, e], kz[0, e], kz[1, e], kb[e]), d)

    def put_weights(x):
        k = kp[x + HALO]
        p = pe[x + 1]
        upper = jnp.where(jnp.logical_and(last, x == LX - 1), 1.0, 0.5)
        lower = jnp.where(jnp.logical_and(first, x == 0), 1.0, 0.5)
        wf[0, x] = (upper * k) * (p - pe[x + 2])
        wf[1, x] = (lower * k) * (p - pe[x])
        wf[2, x] = (inner_y * k) * (p - pltpu.roll(p, NG - 1, 0))
        wf[3, x] = (inner_ym * k) * (p - pltpu.roll(p, 1, 0))
        wf[4, x] = (inner_z * k) * (p - pltpu.roll(p, NG - 1, 1))
        wf[5, x] = (inner_zm * k) * (p - pltpu.roll(p, 1, 1))
        wf[6, x] = kb[x + HALO] * p

    lhs_p = jnp.concatenate(
        [jnp.concatenate([byt[0], byt[0]], axis=1), jnp.concatenate([byt[1], byt[1]], axis=1)], axis=0
    )

    def put_proj(f, layers, ds):
        parts = []
        for x, d in zip(layers, ds):
            grad = weigh(tuple(wf[j, x] for j in range(7)), d)
            parts.append(jnp.concatenate(pieces(grad, 2), axis=0))
        got = mm(lhs_p, jnp.concatenate(parts, axis=1))
        got = got[:M] + got[M:]
        for j, x in enumerate(layers):
            pbuf[f, x] = got[:, j * NG : (j + 1) * NG]

    def put_u0(x, d):
        g = s * LX + x
        safe = jnp.clip(g, 0, NX - 1)
        load = []
        for b in range(8):
            _, cell = sensor_of(safe, b)
            load.append(jnp.where(flat == cell, rsum[x + 2, b : b + 1, :], 0.0))
        u0[x + 2] = jnp.concatenate(load, axis=0) - operator(d, x + HALO)

    def put_u1(x, d):
        u1[x + 1] = operator(d, x + HALO) * tau

    def step_x(layers, project):
        ds = [differences(xe, x + 3) for x in layers]
        for x, d in zip(layers, ds):
            put_u0(x, d)
        if project:
            put_proj(0, layers, ds)

    def step_u0(layers, project):
        ds = [differences(u0, x + 2) for x in layers]
        for x, d in zip(layers, ds):
            put_u1(x, d)
        if project:
            put_proj(1, layers, ds)

    def step_u1(layers, sums):
        ds = [differences(u1, x + 1) for x in layers]
        m0, m1, m2, m3 = sums
        for x, d in zip(layers, ds):
            second, image = d[6], operator(d, x + HALO)
            start = u0[x + 2]
            m0 = m0 + fold(start * start)
            m1 = m1 + fold(start * second)
            m2 = m2 + fold(second * second)
            m3 = m3 + fold(second * image)
        put_proj(2, layers, ds)
        return m0, m1, m2, m3

    def mix_x(layers, fresh):
        def some(j, carry):
            for f in range(3):
                kept = [pbuf[f, x] for x in layers]
                for i in (4 * j, 4 * j + 1, 4 * j + 2, 4 * j + 3):
                    total = None if fresh else qbuf[f, i]
                    for x, part in zip(layers, kept):
                        term = bx_ref[i, s * LX + x] * part
                        total = term if total is None else total + term
                    qbuf[f, i] = total
            return carry

        lax.fori_loop(0, M // 4, some, 0)

    def pairs(lo, hi, step):
        def body(j, carry):
            step((lo + 2 * j, lo + 2 * j + 1))
            return carry

        lax.fori_loop(0, (hi - lo) // 2, body, 0)

    def around(j):
        return j, LX - 1 - j

    load_x.wait()
    pairs(1, LX - 1, lambda layers: [put_weights(x) for x in layers])
    pairs(1, LX - 1, lambda layers: step_x(layers, True))
    pairs(2, LX - 2, lambda layers: step_u0(layers, True))
    zero = jnp.zeros((8, NG), F32)
    sums = lax.fori_loop(
        0, LX // 2 - 3, lambda j, c: step_u1((3 + 2 * j, 4 + 2 * j), c), (zero, zero, zero, zero)
    )
    mix_x(range(3, 13), True)

    load_c.wait()
    pltpu.make_async_copy(cs.at[pl.ds(1, NP - 1)], cs.at[pl.ds(1, NP - 1)], c_recv).wait()
    every = cs[...]
    mine = cs[0]
    gap = every - mine[None]
    near = jnp.sum(jnp.sum(gap * gap, axis=1), axis=1, keepdims=True)
    center = jnp.sum(every, axis=0) * (1.0 / NP)
    off = every - center[None]
    spread = jnp.sum(jnp.sum(off * off, axis=0), keepdims=True) * (2.0 / (NP - 1))
    lane32 = lax.broadcasted_iota(jnp.int32, (NP, NG), 1)
    diag = lane32 == lax.broadcasted_iota(jnp.int32, (NP, NG), 0)
    near_row = jnp.sum(jnp.where(diag, near, 0.0), axis=0, keepdims=True)
    near_row = jnp.where(lane32[0:1] == NP, spread, near_row)
    tail = jnp.concatenate([jnp.broadcast_to(tau, (1, NG)), near_row, jnp.zeros((6, NG), F32)], axis=0)

    @pl.when(jnp.logical_not(first))
    def _():
        x_up().wait_recv()
        r_up().wait_recv()

    @pl.when(jnp.logical_not(last))
    def _():
        x_down().wait_recv()
        r_down().wait_recv()

    @pl.when(jnp.logical_not(first))
    def _():
        p_up().wait_recv()

    @pl.when(jnp.logical_not(last))
    def _():
        p_down().wait_recv()

    for x in around(0):
        put_weights(x)
    step_x(around(-2), False)
    step_x(around(-1), False)
    step_x(around(0), True)

    @pl.when(first)
    def _():
        u0[0:2] = jnp.zeros((2, NG, NG), F32)

    @pl.when(last)
    def _():
        u0[LX + 2 :] = jnp.zeros((2, NG, NG), F32)

    step_u0(around(-1), False)
    step_u0(around(0), True)
    step_u0(around(1), True)

    @pl.when(first)
    def _():
        u1[0:1] = jnp.zeros((1, NG, NG), F32)

    @pl.when(last)
    def _():
        u1[LX + 1 :] = jnp.zeros((1, NG, NG), F32)

    for j in range(3):
        sums = step_u1(around(j), sums)
    mix_x((0, 1, 2, 13, 14, 15), False)

    q_two = jnp.concatenate(pieces(qbuf[...].reshape(3 * M * M, NG), 2), axis=1)
    lhs_z = jnp.concatenate(
        [jnp.concatenate([bzt[0], bzt[0]], axis=1), jnp.concatenate([bzt[1], bzt[1]], axis=1)], axis=0
    )
    tensor = mm_nt(lhs_z, q_two)
    tensor = tensor[:M] + tensor[M:]
    parts = []
    for f in range(3):
        parts += pieces(tensor[:, f * M * M : (f + 1) * M * M], 2)
    rhs = jnp.concatenate(parts, axis=0)

    m3 = sums[3] * tau
    rows = [
        jnp.broadcast_to(jnp.sum(jnp.sum(m, axis=0, keepdims=True), axis=1, keepdims=True), (1, NG))
        for m in (sums[0], sums[1], sums[2], m3)
    ]
    head = jnp.concatenate(rows, axis=0)

    for share in range(NS):
        cols = slice(share * SH, (share + 1) * SH)
        got = mm(rhs, hot[:, cols])
        low = lhot[:, cols]
        for f in range(3):
            at = 2 * M * f
            row = jnp.sum((got[at : at + M] + got[at + M : at + 2 * M]) * low, axis=0, keepdims=True)
            for q in range(SH // NG):
                pk[share, 4 * f + q : 4 * f + q + 1, :] = row[:, q * NG : (q + 1) * NG]
        pk[share, 12:16, :] = head
        pk[share, 16:24, :] = tail

    for j in range(NS - 1):
        r = far(j, NS)
        remote(pk.at[lax.rem(s + r, NS)], rp.at[NS - r], r_send, r_recv, peer_s(r)).start()
    rp[0] = pk[s]
    pltpu.make_async_copy(rp.at[pl.ds(1, NS - 1)], rp.at[pl.ds(1, NS - 1)], r_recv).wait()

    taus = rp[:, 16:17, :]
    least = jnp.min(taus, axis=0)
    ratio = least[None] / taus
    q0 = jnp.sum(rp[:, 12:13, :], axis=0)
    q1 = jnp.sum(rp[:, 13:14, :] * ratio, axis=0)
    q2 = jnp.sum(rp[:, 14:15, :] * (ratio * ratio), axis=0)
    q3 = jnp.sum(rp[:, 15:16, :] * (ratio * ratio * ratio), axis=0)
    proj0 = jnp.sum(rp[:, 0:4, :], axis=0)
    proj1 = jnp.sum(rp[:, 4:8, :], axis=0)
    proj2 = jnp.sum(rp[:, 8:12, :] * ratio, axis=0)
    alpha = q0 / q1
    norm = alpha * alpha * q2 - q0
    grown = norm / q0 + 1.0
    alpha1 = norm / (alpha * alpha * (q3 - q2 * (q2 / q1)))
    tau0 = least
    scale0 = tau0 * (alpha + alpha1 * grown)
    scale2 = -(tau0 * alpha1) * alpha
    gs[0] = proj0 + scale0 * proj1 + scale2 * proj2

    for j in range(NP - 1):
        r = far(j, NP)
        remote(gs.at[0], gs.at[NP - r], g_send, g_recv, peer_p(r)).start()

    scale1 = scale2 * (tau0 / tau)

    def put_x(x, carry):
        adj_ref[x] = xe[x + 3] + scale0 * u0[x + 2] + scale1 * u1[x + 1]
        return carry

    lax.fori_loop(0, LX, put_x, 0)

    near_all = jnp.sum(rp[:, 17:18, :], axis=0)
    width = near_all[:, NP : NP + 1]
    kern = jnp.exp(-near_all / width)
    kcol = jnp.sum(jnp.where(diag, kern, 0.0), axis=1, keepdims=True)
    weight = jnp.broadcast_to(kcol[:, :, None], (NP, 1, NG))
    drive = jnp.sum(weight * every, axis=0)
    repel = jnp.sum(weight * (mine[None] - every), axis=0)
    base = mine + (STEP / NP) * ((2.0 / width) * repel - drive)

    pltpu.make_async_copy(gs.at[pl.ds(1, NP - 1)], gs.at[pl.ds(1, NP - 1)], g_recv).wait()
    new_ref[...] = base - (STEP / NP) * jnp.sum(weight * gs[...], axis=0)

    def sent(ref, sem):
        pltpu.make_async_copy(ref, ref, sem).wait()

    sent(cs.at[pl.ds(1, NP - 1)], c_send)
    sent(rp.at[pl.ds(1, NS - 1)], r_send)
    sent(gs.at[pl.ds(1, NP - 1)], g_send)

    @pl.when(jnp.logical_not(last))
    def _():
        x_up().wait_send()
        p_up().wait_send()
        r_up().wait_send()

    @pl.when(jnp.logical_not(first))
    def _():
        x_down().wait_send()
        p_down().wait_send()
        r_down().wait_send()


def shards(coeffs, modes, basis_x, basis_y, basis_z, pressure, initial_adjoint, sensors, observed, precision):
    vmem = pl.BlockSpec(memory_space=pltpu.VMEM)
    hbm = pl.BlockSpec(memory_space=pltpu.HBM)
    dma = pltpu.SemaphoreType.DMA
    layers = lambda count: pltpu.VMEM((count, NG, NG), F32)
    new, adjoint = pl.pallas_call(
        kernel,
        out_shape=(
            pltpu.VMEM((SH // NG, NG), F32),
            pltpu.VMEM((LX, NG, NG), F32),
        ),
        in_specs=[hbm] * 10,
        out_specs=(vmem, vmem),
        scratch_shapes=[
            pltpu.VMEM((K // NG, NG), jnp.int32),
            pltpu.SMEM((M, NX), F32),
            pltpu.VMEM((M, NG), F32),
            pltpu.VMEM((M, NG), F32),
            pltpu.SMEM(sensors.shape, jnp.int32),
            pltpu.SMEM(sensors.shape, F32),
            pltpu.SMEM(sensors.shape, F32),
            layers(LX + 6),
            layers(LX + 2),
            layers(LX + 6),
            layers(LX + 6),
            pltpu.VMEM((2, LX + 6, NG, NG), F32),
            pltpu.VMEM((2, LX + 6, NG, NG), F32),
            layers(LX + 6),
            pltpu.VMEM((7, LX, NG, NG), F32),
            layers(LX + 4),
            layers(LX + 2),
            pltpu.VMEM((LX + 4, 8, NG), F32),
            pltpu.VMEM((M * M, K), BF16),
            pltpu.VMEM((M, K), F32),
            pltpu.VMEM((3 * M, K), BF16),
            pltpu.VMEM((M, M, NG), F32),
            pltpu.VMEM((3, LX, M, NG), F32),
            pltpu.VMEM((3, M, M, NG), F32),
            pltpu.VMEM((NP, SH // NG, NG), F32),
            pltpu.VMEM((NS, SH // NG, NG), F32),
            pltpu.VMEM((NS, 24, NG), F32),
            pltpu.VMEM((NS, 24, NG), F32),
            pltpu.VMEM((NP, SH // NG, NG), F32),
            dma((3,)), dma((7,)), dma((6,)), dma((6,)),
            dma, dma, dma, dma, dma, dma, dma,
        ],
        compiler_params=pltpu.CompilerParams(
            collective_id=0, has_side_effects=True, vmem_limit_bytes=60 * 2**20
        ),
    )(
        coeffs.reshape(NS, SH // NG, NG),
        modes.reshape(K // NG, NG),
        basis_x.T,
        basis_y.T,
        basis_z.T,
        pressure[0],
        initial_adjoint[0],
        sensors,
        observed,
        precision,
    )
    return new.reshape(1, SH), adjoint[None]


def solution(mesh):
    in_specs = (
        P("particle", None),
        P(),
        P(),
        P(),
        P(),
        P("particle", "space", None, None),
        P("particle", "space", None, None),
        P(),
        P(),
        P(),
    )
    out_specs = (P("particle", "space"), P("particle", "space", None, None))
    return jax.shard_map(shards, mesh=mesh, in_specs=in_specs, out_specs=out_specs, check_vma=False)
```

```python
import jax
import jax.numpy as jnp
from jax import lax
from jax.experimental import pallas as pl
from jax.experimental.pallas import tpu as pltpu
from jax.sharding import PartitionSpec as P

F32 = jnp.float32
BF16 = jnp.bfloat16
NP = 32
NS = 8
LX = 16
NX = 128
NG = 128
M = 16
K = M * M * M
SH = K // NS
HALO = 3
STEP = 0.5
NN = (((1,), (1,)), ((), ()))


def pieces(value, count):
    out = []
    rest = value
    for _ in range(count):
        part = rest.astype(BF16)
        out.append(part)
        rest = rest - part.astype(F32)
    return out


def mm(a, b):
    return jnp.dot(a, b, preferred_element_type=F32)


def mm_nt(a, b):
    return lax.dot_general(a, b, NN, preferred_element_type=F32)


def fold(value):
    return jnp.sum(value.reshape(NG // 8, 8, NG), axis=0)


def kernel(
    c_hbm, modes_in, bx_in, by_in, bz_in, p_hbm, x_hbm, sens_in, obs_in, prec_in,
    new_ref, adj_ref,
    modes_ref, bx_ref, by_ref, bz_ref, sens_ref, obs_ref, prec_ref, xe, pe, kp, kx, ky, kz, kb, wf, u0, u1, rsum, hot, lhot, lcs, fbuf, pbuf, qbuf,
    cs, wk, pk, rp, gs,
    in_sem, small_sem, halo_send, halo_recv, c_own, c_send, c_recv, r_send, r_recv, g_send, g_recv,
):
    n = lax.axis_index("particle")
    s = lax.axis_index("space")
    first = s == 0
    last = s == NS - 1

    def far(j, count):
        half = (j + 1) // 2
        return count // 2 + (half if j % 2 else -half)

    def peer_p(r):
        return {"particle": lax.rem(n + r, NP)}

    def peer_s(r):
        return {"space": lax.rem(s + r, NS)}

    barrier = pltpu.get_barrier_semaphore()

    load_x = pltpu.make_async_copy(x_hbm, xe.at[pl.ds(HALO, LX)], in_sem.at[0])
    load_p = pltpu.make_async_copy(p_hbm, pe.at[pl.ds(1, LX)], in_sem.at[1])
    load_c = pltpu.make_async_copy(c_hbm.at[s], cs.at[0], c_own)
    load_all = pltpu.make_async_copy(c_hbm, wk, in_sem.at[2])
    small = (
        (modes_in, modes_ref), (bx_in, bx_ref), (by_in, by_ref), (bz_in, bz_ref),
        (sens_in, sens_ref), (obs_in, obs_ref), (prec_in, prec_ref),
    )
    load_small = [pltpu.make_async_copy(src, dst, small_sem.at[j]) for j, (src, dst) in enumerate(small)]
    load_all.start()
    load_small[0].start()

    for j in range(NP - 1):
        pl.semaphore_signal(barrier, inc=1, device_id=peer_p(far(j, NP)))
    for r in range(1, NS):
        pl.semaphore_signal(barrier, inc=1, device_id=peer_s(r))

    for load in load_small[1:]:
        load.start()
    load_p.start()
    load_x.start()
    load_c.start()

    load_all.wait()
    load_small[0].wait()
    row_id = lax.broadcasted_iota(jnp.int32, (M * M, NG), 0)
    sub_id = lax.broadcasted_iota(jnp.int32, (M, NG), 0)
    for chunk in range(K // NG):
        pos = modes_ref[chunk : chunk + 1, :]
        cols = slice(chunk * NG, (chunk + 1) * NG)
        upper = lax.shift_right_logical(pos, 4)
        lower = lax.bitwise_and(pos, 15)
        hot[:, cols] = jnp.where(row_id == upper, 1.0, 0.0).astype(BF16)
        low = jnp.where(sub_id == lower, 1.0, 0.0)
        lhot[:, cols] = low
        own = wk[chunk // 4, chunk % 4 : chunk % 4 + 1, :]
        for q, part in enumerate(pieces(own, 3)):
            lcs[q * M : (q + 1) * M, cols] = (low * part.astype(F32)).astype(BF16)

    lane = lax.broadcasted_iota(jnp.int32, (NG, NG), 1)
    suby = lax.broadcasted_iota(jnp.int32, (NG, NG), 0)
    eye = jnp.where(lane == suby, 1.0, 0.0).astype(BF16)
    for load in load_small[1:4]:
        load.wait()
    byt = pieces(by_ref[...], 3)
    bzt = pieces(bz_ref[...], 3)
    lhs_y = mm_nt(eye, jnp.concatenate([byt[which] for which in (0, 0, 1, 0, 1, 2)], axis=0)).astype(BF16)

    xi = mm_nt(hot[...], lcs[...]).astype(BF16)
    field = mm(xi, jnp.concatenate([bzt[0]] * 3, axis=0))
    field = field + mm(xi, jnp.concatenate([bzt[1]] * 3, axis=0))
    field = field + mm(xi, jnp.concatenate([bzt[2]] * 3, axis=0))
    fbuf[...] = field.reshape(M, M, NG)

    inner_y = jnp.where(suby == NG - 1, 0.0, 0.5)
    inner_z = jnp.where(lane == NG - 1, 0.0, 0.5)
    inner_ym = jnp.where(suby == 0, 0.0, 0.5)
    inner_zm = jnp.where(lane == 0, 0.0, 0.5)
    rim = (
        jnp.where(suby == NG - 1, 1.0, 0.0)
        + jnp.where(suby == 0, 1.0, 0.0)
        + jnp.where(lane == NG - 1, 1.0, 0.0)
        + jnp.where(lane == 0, 1.0, 0.0)
    )

    def mix(e):
        g = jnp.clip(s * LX - HALO + e, 0, NX - 1)
        total = bx_ref[0, g] * fbuf[0]
        for i in range(1, M):
            total = total + bx_ref[i, g] * fbuf[i]
        a, b, c = pieces(total, 3)
        return jnp.concatenate([a, b, a, c, b, a], axis=0)

    def faces(e, k, before):
        kp[e] = k
        ky[0, e] = inner_y * (k + pltpu.roll(k, NG - 1, 0))
        kz[0, e] = inner_z * (k + pltpu.roll(k, NG - 1, 1))
        ky[1, e] = inner_ym * (k + pltpu.roll(k, 1, 0))
        kz[1, e] = inner_zm * (k + pltpu.roll(k, 1, 1))
        kb[e] = rim * k
        kx[before] = 0.5 * (kp[before] + k)

    def log_layers(t, top):
        e = 2 * t
        both = jnp.exp(mm(lhs_y, jnp.concatenate([mix(e), mix(e + 1)], axis=1)))
        k0, k1 = both[:, :NG], both[:, NG:]
        faces(e, k0, max(e - 1, 0))
        faces(e + 1, k1, e)
        return jnp.maximum(top, jnp.max(jnp.maximum(k0, k1).reshape(NG // 8, 8, NG), axis=0))

    top = jnp.zeros((8, NG), F32)
    for t in range(HALO + LX // 2):
        top = log_layers(t, top)
    tau = (1.0 / 16.0) / jnp.max(top, keepdims=True)

    @pl.when(first)
    def _():
        xe[0:HALO] = jnp.zeros((HALO, NG, NG), F32)
        pe[0:1] = jnp.zeros((1, NG, NG), F32)
        rsum[0:2] = jnp.zeros((2, 8, NG), F32)

    @pl.when(last)
    def _():
        xe[HALO + LX :] = jnp.zeros((HALO, NG, NG), F32)
        pe[LX + 1 :] = jnp.zeros((1, NG, NG), F32)
        rsum[LX + 2 :] = jnp.zeros((2, 8, NG), F32)

    pl.semaphore_wait(barrier, NS - 1 + NP - 1)

    up = {"space": jnp.minimum(s + 1, NS - 1)}
    down = {"space": jnp.maximum(s - 1, 0)}

    def remote(src, dst, send, recv, where):
        return pltpu.make_async_remote_copy(src_ref=src, dst_ref=dst, send_sem=send, recv_sem=recv, device_id=where)

    def x_up():
        return remote(x_hbm.at[pl.ds(LX - HALO, HALO)], xe.at[pl.ds(0, HALO)], halo_send.at[0], halo_recv.at[0], up)

    def x_down():
        return remote(x_hbm.at[pl.ds(0, HALO)], xe.at[pl.ds(HALO + LX, HALO)], halo_send.at[1], halo_recv.at[1], down)

    def p_up():
        return remote(p_hbm.at[pl.ds(LX - 1, 1)], pe.at[pl.ds(0, 1)], halo_send.at[2], halo_recv.at[2], up)

    def p_down():
        return remote(p_hbm.at[pl.ds(0, 1)], pe.at[pl.ds(LX + 1, 1)], halo_send.at[3], halo_recv.at[3], down)

    def r_up():
        return remote(rsum.at[pl.ds(LX, 2)], rsum.at[pl.ds(0, 2)], halo_send.at[4], halo_recv.at[4], up)

    def r_down():
        return remote(rsum.at[pl.ds(2, 2)], rsum.at[pl.ds(LX + 2, 2)], halo_send.at[5], halo_recv.at[5], down)

    @pl.when(jnp.logical_not(last))
    def _():
        x_up().start()

    @pl.when(jnp.logical_not(first))
    def _():
        x_down().start()

    @pl.when(jnp.logical_not(last))
    def _():
        p_up().start()

    @pl.when(jnp.logical_not(first))
    def _():
        p_down().start()

    def send_c(r, carry):
        remote(c_hbm.at[s], cs.at[NP - r], c_send, c_recv, peer_p(r)).start()
        return carry

    flat = (
        lax.broadcasted_iota(jnp.int32, (M, NG), 0) * NG + lax.broadcasted_iota(jnp.int32, (M, NG), 1)
    )

    def sensor_of(layer, block):
        index = layer * 8 + block
        return index, sens_ref[index] - index * (M * NG)

    load_p.wait()
    for load in load_small[4:]:
        load.wait()

    def misfit(x, carry):
        for b in range(8):
            index, cell = sensor_of(s * LX + x, b)
            part = pe[x + 1, b * M : (b + 1) * M, :]
            hit = jnp.where(flat == cell, (part - obs_ref[index]) * prec_ref[index], 0.0)
            rsum[x + 2, b : b + 1, :] = jnp.sum(hit, axis=0, keepdims=True)
        return carry

    lax.fori_loop(0, LX, misfit, 0)

    @pl.when(jnp.logical_not(last))
    def _():
        r_up().start()

    @pl.when(jnp.logical_not(first))
    def _():
        r_down().start()

    lax.fori_loop(1, NP, send_c, 0)

    def differences(v_ref, i):
        v = v_ref[i]
        return (
            v - v_ref[i + 1],
            v - v_ref[i - 1],
            v - pltpu.roll(v, NG - 1, 0),
            v - pltpu.roll(v, 1, 0),
            v - pltpu.roll(v, NG - 1, 1),
            v - pltpu.roll(v, 1, 1),
            v,
        )

    def weigh(weights, parts):
        total = weights[0] * parts[0]
        for weight, part in zip(weights[1:], parts[1:]):
            total = total + weight * part
        return total

    def operator(d, e):
        return weigh((kx[e], kx[e - 1], ky[0, e], ky[1, e], kz[0, e], kz[1, e], kb[e]), d)

    def put_weights(x):
        k = kp[x + HALO]
        p = pe[x + 1]
        upper = jnp.where(jnp.logical_and(last, x == LX - 1), 1.0, 0.5)
        lower = jnp.where(jnp.logical_and(first, x == 0), 1.0, 0.5)
        wf[0, x] = (upper * k) * (p - pe[x + 2])
        wf[1, x] = (lower * k) * (p - pe[x])
        wf[2, x] = (inner_y * k) * (p - pltpu.roll(p, NG - 1, 0))
        wf[3, x] = (inner_ym * k) * (p - pltpu.roll(p, 1, 0))
        wf[4, x] = (inner_z * k) * (p - pltpu.roll(p, NG - 1, 1))
        wf[5, x] = (inner_zm * k) * (p - pltpu.roll(p, 1, 1))
        wf[6, x] = kb[x + HALO] * p

    lhs_p = jnp.concatenate(
        [jnp.concatenate([byt[0], byt[0]], axis=1), jnp.concatenate([byt[1], byt[1]], axis=1)], axis=0
    )

    def put_proj(f, layers, ds):
        parts = []
        for x, d in zip(layers, ds):
            grad = weigh(tuple(wf[j, x] for j in range(7)), d)
            parts.append(jnp.concatenate(pieces(grad, 2), axis=0))
        got = mm(lhs_p, jnp.concatenate(parts, axis=1))
        got = got[:M] + got[M:]
        for j, x in enumerate(layers):
            pbuf[f, x] = got[:, j * NG : (j + 1) * NG]

    def put_u0(x, d):
        g = s * LX + x
        safe = jnp.clip(g, 0, NX - 1)
        load = []
        for b in range(8):
            _, cell = sensor_of(safe, b)
            load.append(jnp.where(flat == cell, rsum[x + 2, b : b + 1, :], 0.0))
        u0[x + 2] = jnp.concatenate(load, axis=0) - operator(d, x + HALO)

    def put_u1(x, d):
        u1[x + 1] = operator(d, x + HALO) * tau

    def step_x(layers, project):
        ds = [differences(xe, x + 3) for x in layers]
        for x, d in zip(layers, ds):
            put_u0(x, d)
        if project:
            put_proj(0, layers, ds)

    def step_u0(layers, project):
        ds = [differences(u0, x + 2) for x in layers]
        for x, d in zip(layers, ds):
            put_u1(x, d)
        if project:
            put_proj(1, layers, ds)

    def step_u1(layers, sums):
        ds = [differences(u1, x + 1) for x in layers]
        m0, m1, m2, m3 = sums
        for x, d in zip(layers, ds):
            second, image = d[6], operator(d, x + HALO)
            start = u0[x + 2]
            m0 = m0 + fold(start * start)
            m1 = m1 + fold(start * second)
            m2 = m2 + fold(second * second)
            m3 = m3 + fold(second * image)
        put_proj(2, layers, ds)
        return m0, m1, m2, m3

    def mix_x(layers, fresh):
        def some(j, carry):
            for f in range(3):
                kept = [pbuf[f, x] for x in layers]
                for i in (4 * j, 4 * j + 1, 4 * j + 2, 4 * j + 3):
                    total = None if fresh else qbuf[f, i]
                    for x, part in zip(layers, kept):
                        term = bx_ref[i, s * LX + x] * part
                        total = term if total is None else total + term
                    qbuf[f, i] = total
            return carry

        lax.fori_loop(0, M // 4, some, 0)

    def pairs(lo, hi, step, wide=2):
        def body(j, carry):
            step(tuple(lo + wide * j + i for i in range(wide)))
            return carry

        lax.fori_loop(0, (hi - lo) // wide, body, 0)

    def around(j):
        return j, LX - 1 - j

    load_x.wait()
    pairs(1, LX - 1, lambda layers: [put_weights(x) for x in layers])
    pairs(1, LX - 1, lambda layers: step_x(layers, True))
    pairs(2, LX - 2, lambda layers: step_u0(layers, True), 4)
    zero = jnp.zeros((8, NG), F32)
    sums = lax.fori_loop(
        0, LX // 2 - 3, lambda j, c: step_u1((3 + 2 * j, 4 + 2 * j), c), (zero, zero, zero, zero)
    )
    mix_x(range(3, 13), True)

    load_c.wait()
    pltpu.make_async_copy(cs.at[pl.ds(1, NP - 1)], cs.at[pl.ds(1, NP - 1)], c_recv).wait()
    every = cs[...]
    mine = cs[0]
    gap = every - mine[None]
    near = jnp.sum(jnp.sum(gap * gap, axis=1), axis=1, keepdims=True)
    center = jnp.sum(every, axis=0) * (1.0 / NP)
    off = every - center[None]
    spread = jnp.sum(jnp.sum(off * off, axis=0), keepdims=True) * (2.0 / (NP - 1))
    lane32 = lax.broadcasted_iota(jnp.int32, (NP, NG), 1)
    diag = lane32 == lax.broadcasted_iota(jnp.int32, (NP, NG), 0)
    near_row = jnp.sum(jnp.where(diag, near, 0.0), axis=0, keepdims=True)
    near_row = jnp.where(lane32[0:1] == NP, spread, near_row)
    tail = jnp.concatenate([jnp.broadcast_to(tau, (1, NG)), near_row, jnp.zeros((6, NG), F32)], axis=0)

    @pl.when(jnp.logical_not(first))
    def _():
        x_up().wait_recv()
        r_up().wait_recv()

    @pl.when(jnp.logical_not(last))
    def _():
        x_down().wait_recv()
        r_down().wait_recv()

    @pl.when(jnp.logical_not(first))
    def _():
        p_up().wait_recv()

    @pl.when(jnp.logical_not(last))
    def _():
        p_down().wait_recv()

    for x in around(0):
        put_weights(x)
    step_x(around(-2), False)
    step_x(around(-1), False)
    step_x(around(0), True)

    @pl.when(first)
    def _():
        u0[0:2] = jnp.zeros((2, NG, NG), F32)

    @pl.when(last)
    def _():
        u0[LX + 2 :] = jnp.zeros((2, NG, NG), F32)

    step_u0(around(-1), False)
    step_u0(around(0), True)
    step_u0(around(1), True)

    @pl.when(first)
    def _():
        u1[0:1] = jnp.zeros((1, NG, NG), F32)

    @pl.when(last)
    def _():
        u1[LX + 1 :] = jnp.zeros((1, NG, NG), F32)

    for j in range(3):
        sums = step_u1(around(j), sums)
    mix_x((0, 1, 2, 13, 14, 15), False)

    q_two = jnp.concatenate(pieces(qbuf[...].reshape(3 * M * M, NG), 2), axis=1)
    lhs_z = jnp.concatenate(
        [jnp.concatenate([bzt[0], bzt[0]], axis=1), jnp.concatenate([bzt[1], bzt[1]], axis=1)], axis=0
    )
    tensor = mm_nt(lhs_z, q_two)
    tensor = tensor[:M] + tensor[M:]
    parts = []
    for f in range(3):
        parts += pieces(tensor[:, f * M * M : (f + 1) * M * M], 2)
    rhs = jnp.concatenate(parts, axis=0)

    m3 = sums[3] * tau
    rows = [
        jnp.broadcast_to(jnp.sum(jnp.sum(m, axis=0, keepdims=True), axis=1, keepdims=True), (1, NG))
        for m in (sums[0], sums[1], sums[2], m3)
    ]
    head = jnp.concatenate(rows, axis=0)

    for share in range(NS):
        cols = slice(share * SH, (share + 1) * SH)
        got = mm(rhs, hot[:, cols])
        low = lhot[:, cols]
        for f in range(3):
            at = 2 * M * f
            row = jnp.sum((got[at : at + M] + got[at + M : at + 2 * M]) * low, axis=0, keepdims=True)
            for q in range(SH // NG):
                pk[share, 4 * f + q : 4 * f + q + 1, :] = row[:, q * NG : (q + 1) * NG]
        pk[share, 12:16, :] = head
        pk[share, 16:24, :] = tail

        @pl.when(s != share)
        def _():
            to = rp.at[lax.rem(s - share + NS, NS)]
            remote(pk.at[share], to, r_send, r_recv, {"space": share}).start()


    rp[0] = pk[s]
    pltpu.make_async_copy(rp.at[pl.ds(1, NS - 1)], rp.at[pl.ds(1, NS - 1)], r_recv).wait()

    taus = rp[:, 16:17, :]
    least = jnp.min(taus, axis=0)
    ratio = least[None] / taus
    q0 = jnp.sum(rp[:, 12:13, :], axis=0)
    q1 = jnp.sum(rp[:, 13:14, :] * ratio, axis=0)
    q2 = jnp.sum(rp[:, 14:15, :] * (ratio * ratio), axis=0)
    q3 = jnp.sum(rp[:, 15:16, :] * (ratio * ratio * ratio), axis=0)
    proj0 = jnp.sum(rp[:, 0:4, :], axis=0)
    proj1 = jnp.sum(rp[:, 4:8, :], axis=0)
    proj2 = jnp.sum(rp[:, 8:12, :] * ratio, axis=0)
    alpha = q0 / q1
    norm = alpha * alpha * q2 - q0
    grown = norm / q0 + 1.0
    alpha1 = norm / (alpha * alpha * (q3 - q2 * (q2 / q1)))
    tau0 = least
    scale0 = tau0 * (alpha + alpha1 * grown)
    scale2 = -(tau0 * alpha1) * alpha
    gs[0] = proj0 + scale0 * proj1 + scale2 * proj2

    for j in range(NP - 1):
        r = far(j, NP)
        remote(gs.at[0], gs.at[NP - r], g_send, g_recv, peer_p(r)).start()

    scale1 = scale2 * (tau0 / tau)

    def put_x(x, carry):
        adj_ref[x] = xe[x + 3] + scale0 * u0[x + 2] + scale1 * u1[x + 1]
        return carry

    lax.fori_loop(0, LX, put_x, 0)

    near_all = jnp.sum(rp[:, 17:18, :], axis=0)
    width = near_all[:, NP : NP + 1]
    kern = jnp.exp(-near_all / width)
    kcol = jnp.sum(jnp.where(diag, kern, 0.0), axis=1, keepdims=True)
    weight = jnp.broadcast_to(kcol[:, :, None], (NP, 1, NG))
    drive = jnp.sum(weight * every, axis=0)
    repel = jnp.sum(weight * (mine[None] - every), axis=0)
    base = mine + (STEP / NP) * ((2.0 / width) * repel - drive)

    pltpu.make_async_copy(gs.at[pl.ds(1, NP - 1)], gs.at[pl.ds(1, NP - 1)], g_recv).wait()
    new_ref[...] = base - (STEP / NP) * jnp.sum(weight * gs[...], axis=0)

    def sent(ref, sem):
        pltpu.make_async_copy(ref, ref, sem).wait()

    sent(cs.at[pl.ds(1, NP - 1)], c_send)
    sent(rp.at[pl.ds(1, NS - 1)], r_send)
    sent(gs.at[pl.ds(1, NP - 1)], g_send)

    @pl.when(jnp.logical_not(last))
    def _():
        x_up().wait_send()
        p_up().wait_send()
        r_up().wait_send()

    @pl.when(jnp.logical_not(first))
    def _():
        x_down().wait_send()
        p_down().wait_send()
        r_down().wait_send()


def shards(coeffs, modes, basis_x, basis_y, basis_z, pressure, initial_adjoint, sensors, observed, precision):
    vmem = pl.BlockSpec(memory_space=pltpu.VMEM)
    hbm = pl.BlockSpec(memory_space=pltpu.HBM)
    dma = pltpu.SemaphoreType.DMA
    layers = lambda count: pltpu.VMEM((count, NG, NG), F32)
    new, adjoint = pl.pallas_call(
        kernel,
        out_shape=(
            pltpu.VMEM((SH // NG, NG), F32),
            pltpu.VMEM((LX, NG, NG), F32),
        ),
        in_specs=[hbm] * 10,
        out_specs=(vmem, vmem),
        scratch_shapes=[
            pltpu.VMEM((K // NG, NG), jnp.int32),
            pltpu.SMEM((M, NX), F32),
            pltpu.VMEM((M, NG), F32),
            pltpu.VMEM((M, NG), F32),
            pltpu.SMEM(sensors.shape, jnp.int32),
            pltpu.SMEM(sensors.shape, F32),
            pltpu.SMEM(sensors.shape, F32),
            layers(LX + 6),
            layers(LX + 2),
            layers(LX + 6),
            layers(LX + 6),
            pltpu.VMEM((2, LX + 6, NG, NG), F32),
            pltpu.VMEM((2, LX + 6, NG, NG), F32),
            layers(LX + 6),
            pltpu.VMEM((7, LX, NG, NG), F32),
            layers(LX + 4),
            layers(LX + 2),
            pltpu.VMEM((LX + 4, 8, NG), F32),
            pltpu.VMEM((M * M, K), BF16),
            pltpu.VMEM((M, K), F32),
            pltpu.VMEM((3 * M, K), BF16),
            pltpu.VMEM((M, M, NG), F32),
            pltpu.VMEM((3, LX, M, NG), F32),
            pltpu.VMEM((3, M, M, NG), F32),
            pltpu.VMEM((NP, SH // NG, NG), F32),
            pltpu.VMEM((NS, SH // NG, NG), F32),
            pltpu.VMEM((NS, 24, NG), F32),
            pltpu.VMEM((NS, 24, NG), F32),
            pltpu.VMEM((NP, SH // NG, NG), F32),
            dma((3,)), dma((7,)), dma((6,)), dma((6,)),
            dma, dma, dma, dma, dma, dma, dma,
        ],
        compiler_params=pltpu.CompilerParams(
            collective_id=0, has_side_effects=True, vmem_limit_bytes=60 * 2**20
        ),
    )(
        coeffs.reshape(NS, SH // NG, NG),
        modes.reshape(K // NG, NG),
        basis_x.T,
        basis_y.T,
        basis_z.T,
        pressure[0],
        initial_adjoint[0],
        sensors,
        observed,
        precision,
    )
    return new.reshape(1, SH), adjoint[None]


def solution(mesh):
    in_specs = (
        P("particle", None),
        P(),
        P(),
        P(),
        P(),
        P("particle", "space", None, None),
        P("particle", "space", None, None),
        P(),
        P(),
        P(),
    )
    out_specs = (P("particle", "space"), P("particle", "space", None, None))
    return jax.shard_map(shards, mesh=mesh, in_specs=in_specs, out_specs=out_specs, check_vma=False)
```

```python
import jax
import jax.numpy as jnp
from jax import lax
from jax.experimental import pallas as pl
from jax.experimental.pallas import tpu as pltpu
from jax.sharding import PartitionSpec as P

F32 = jnp.float32
BF16 = jnp.bfloat16
NP = 32
NS = 8
LX = 16
NX = 128
NG = 128
M = 16
K = M * M * M
SH = K // NS
HALO = 3
STEP = 0.5
NN = (((1,), (1,)), ((), ()))


def pieces(value, count):
    out = []
    rest = value
    for _ in range(count):
        part = rest.astype(BF16)
        out.append(part)
        rest = rest - part.astype(F32)
    return out


def mm(a, b):
    return jnp.dot(a, b, preferred_element_type=F32)


def mm_nt(a, b):
    return lax.dot_general(a, b, NN, preferred_element_type=F32)


def fold(value):
    return jnp.sum(value.reshape(NG // 8, 8, NG), axis=0)


def kernel(
    c_hbm, modes_in, bx_in, by_in, bz_in, p_hbm, x_hbm, sens_in, obs_in, prec_in,
    new_ref, adj_ref,
    modes_ref, bx_ref, by_ref, bz_ref, sens_ref, obs_ref, prec_ref, xe, pe, kp, kx, ky, kz, kb, wf, u0, u1, rsum, hot, lhot, lcs, fbuf, pbuf, qbuf,
    cs, wk, pk, rp, gs,
    in_sem, small_sem, halo_send, halo_recv, c_own, c_send, c_recv, r_send, r_recv, g_send, g_recv,
):
    n = lax.axis_index("particle")
    s = lax.axis_index("space")
    first = s == 0
    last = s == NS - 1

    def far(j, count):
        half = (j + 1) // 2
        return count // 2 + (half if j % 2 else -half)

    def peer_p(r):
        return {"particle": lax.rem(n + r, NP)}

    def peer_s(r):
        return {"space": lax.rem(s + r, NS)}

    barrier = pltpu.get_barrier_semaphore()

    load_x = pltpu.make_async_copy(x_hbm, xe.at[pl.ds(HALO, LX)], in_sem.at[0])
    load_p = pltpu.make_async_copy(p_hbm, pe.at[pl.ds(1, LX)], in_sem.at[1])
    load_c = pltpu.make_async_copy(c_hbm.at[s], cs.at[0], c_own)
    load_all = pltpu.make_async_copy(c_hbm, wk, in_sem.at[2])
    small = (
        (modes_in, modes_ref), (bx_in, bx_ref), (by_in, by_ref), (bz_in, bz_ref),
        (sens_in, sens_ref), (obs_in, obs_ref), (prec_in, prec_ref),
    )
    load_small = [pltpu.make_async_copy(src, dst, small_sem.at[j]) for j, (src, dst) in enumerate(small)]
    load_all.start()
    load_small[0].start()

    for j in range(NP - 1):
        pl.semaphore_signal(barrier, inc=1, device_id=peer_p(far(j, NP)))
    for r in range(1, NS):
        pl.semaphore_signal(barrier, inc=1, device_id=peer_s(r))

    for load in load_small[1:]:
        load.start()
    load_p.start()
    load_x.start()
    load_c.start()

    load_all.wait()
    load_small[0].wait()
    row_id = lax.broadcasted_iota(jnp.int32, (M * M, NG), 0)
    sub_id = lax.broadcasted_iota(jnp.int32, (M, NG), 0)
    for chunk in range(K // NG):
        pos = modes_ref[chunk : chunk + 1, :]
        cols = slice(chunk * NG, (chunk + 1) * NG)
        upper = lax.shift_right_logical(pos, 4)
        lower = lax.bitwise_and(pos, 15)
        hot[:, cols] = jnp.where(row_id == upper, 1.0, 0.0).astype(BF16)
        low = jnp.where(sub_id == lower, 1.0, 0.0)
        lhot[:, cols] = low
        own = wk[chunk // 4, chunk % 4 : chunk % 4 + 1, :]
        for q, part in enumerate(pieces(own, 3)):
            lcs[q * M : (q + 1) * M, cols] = (low * part.astype(F32)).astype(BF16)

    lane = lax.broadcasted_iota(jnp.int32, (NG, NG), 1)
    suby = lax.broadcasted_iota(jnp.int32, (NG, NG), 0)
    eye = jnp.where(lane == suby, 1.0, 0.0).astype(BF16)
    for load in load_small[1:4]:
        load.wait()
    byt = pieces(by_ref[...], 3)
    bzt = pieces(bz_ref[...], 3)
    lhs_y = mm_nt(eye, jnp.concatenate([byt[which] for which in (0, 0, 1, 0, 1, 2)], axis=0)).astype(BF16)

    xi = mm_nt(hot[...], lcs[...]).astype(BF16)
    field = mm(xi, jnp.concatenate([bzt[0]] * 3, axis=0))
    field = field + mm(xi, jnp.concatenate([bzt[1]] * 3, axis=0))
    field = field + mm(xi, jnp.concatenate([bzt[2]] * 3, axis=0))
    fbuf[...] = field.reshape(M, M, NG)

    inner_y = jnp.where(suby == NG - 1, 0.0, 0.5)
    inner_z = jnp.where(lane == NG - 1, 0.0, 0.5)
    inner_ym = jnp.where(suby == 0, 0.0, 0.5)
    inner_zm = jnp.where(lane == 0, 0.0, 0.5)
    rim = (
        jnp.where(suby == NG - 1, 1.0, 0.0)
        + jnp.where(suby == 0, 1.0, 0.0)
        + jnp.where(lane == NG - 1, 1.0, 0.0)
        + jnp.where(lane == 0, 1.0, 0.0)
    )

    def mix(e):
        g = jnp.clip(s * LX - HALO + e, 0, NX - 1)
        total = bx_ref[0, g] * fbuf[0]
        for i in range(1, M):
            total = total + bx_ref[i, g] * fbuf[i]
        a, b, c = pieces(total, 3)
        return jnp.concatenate([a, b, a, c, b, a], axis=0)

    def faces(e, k, before):
        kp[e] = k
        ky[0, e] = inner_y * (k + pltpu.roll(k, NG - 1, 0))
        kz[0, e] = inner_z * (k + pltpu.roll(k, NG - 1, 1))
        ky[1, e] = inner_ym * (k + pltpu.roll(k, 1, 0))
        kz[1, e] = inner_zm * (k + pltpu.roll(k, 1, 1))
        kb[e] = rim * k
        kx[before] = 0.5 * (kp[before] + k)

    def log_layers(t, top):
        e = 2 * t
        both = jnp.exp(mm(lhs_y, jnp.concatenate([mix(e), mix(e + 1)], axis=1)))
        k0, k1 = both[:, :NG], both[:, NG:]
        faces(e, k0, max(e - 1, 0))
        faces(e + 1, k1, e)
        return jnp.maximum(top, jnp.max(jnp.maximum(k0, k1).reshape(NG // 8, 8, NG), axis=0))

    top = jnp.zeros((8, NG), F32)
    for t in range(HALO + LX // 2):
        top = log_layers(t, top)
    tau = (1.0 / 16.0) / jnp.max(top, keepdims=True)

    @pl.when(first)
    def _():
        xe[0:HALO] = jnp.zeros((HALO, NG, NG), F32)
        pe[0:1] = jnp.zeros((1, NG, NG), F32)
        rsum[0:2] = jnp.zeros((2, 8, NG), F32)

    @pl.when(last)
    def _():
        xe[HALO + LX :] = jnp.zeros((HALO, NG, NG), F32)
        pe[LX + 1 :] = jnp.zeros((1, NG, NG), F32)
        rsum[LX + 2 :] = jnp.zeros((2, 8, NG), F32)

    pl.semaphore_wait(barrier, NS - 1 + NP - 1)

    up = {"space": jnp.minimum(s + 1, NS - 1)}
    down = {"space": jnp.maximum(s - 1, 0)}

    def remote(src, dst, send, recv, where):
        return pltpu.make_async_remote_copy(src_ref=src, dst_ref=dst, send_sem=send, recv_sem=recv, device_id=where)

    def x_up():
        return remote(x_hbm.at[pl.ds(LX - HALO, HALO)], xe.at[pl.ds(0, HALO)], halo_send.at[0], halo_recv.at[0], up)

    def x_down():
        return remote(x_hbm.at[pl.ds(0, HALO)], xe.at[pl.ds(HALO + LX, HALO)], halo_send.at[1], halo_recv.at[1], down)

    def p_up():
        return remote(p_hbm.at[pl.ds(LX - 1, 1)], pe.at[pl.ds(0, 1)], halo_send.at[2], halo_recv.at[2], up)

    def p_down():
        return remote(p_hbm.at[pl.ds(0, 1)], pe.at[pl.ds(LX + 1, 1)], halo_send.at[3], halo_recv.at[3], down)

    def r_up():
        return remote(rsum.at[pl.ds(LX, 2)], rsum.at[pl.ds(0, 2)], halo_send.at[4], halo_recv.at[4], up)

    def r_down():
        return remote(rsum.at[pl.ds(2, 2)], rsum.at[pl.ds(LX + 2, 2)], halo_send.at[5], halo_recv.at[5], down)

    @pl.when(jnp.logical_not(last))
    def _():
        x_up().start()

    @pl.when(jnp.logical_not(first))
    def _():
        x_down().start()

    @pl.when(jnp.logical_not(last))
    def _():
        p_up().start()

    @pl.when(jnp.logical_not(first))
    def _():
        p_down().start()

    def send_c(r, carry):
        remote(c_hbm.at[s], cs.at[NP - r], c_send, c_recv, peer_p(r)).start()
        return carry

    flat = (
        lax.broadcasted_iota(jnp.int32, (M, NG), 0) * NG + lax.broadcasted_iota(jnp.int32, (M, NG), 1)
    )

    def sensor_of(layer, block):
        index = layer * 8 + block
        return index, sens_ref[index] - index * (M * NG)

    load_p.wait()
    for load in load_small[4:]:
        load.wait()

    def misfit(x, carry):
        for b in range(8):
            index, cell = sensor_of(s * LX + x, b)
            part = pe[x + 1, b * M : (b + 1) * M, :]
            hit = jnp.where(flat == cell, (part - obs_ref[index]) * prec_ref[index], 0.0)
            rsum[x + 2, b : b + 1, :] = jnp.sum(hit, axis=0, keepdims=True)
        return carry

    lax.fori_loop(0, LX, misfit, 0)

    @pl.when(jnp.logical_not(last))
    def _():
        r_up().start()

    @pl.when(jnp.logical_not(first))
    def _():
        r_down().start()

    lax.fori_loop(1, NP, send_c, 0)

    def differences(v_ref, i):
        v = v_ref[i]
        return (
            v - v_ref[i + 1],
            v - v_ref[i - 1],
            v - pltpu.roll(v, NG - 1, 0),
            v - pltpu.roll(v, 1, 0),
            v - pltpu.roll(v, NG - 1, 1),
            v - pltpu.roll(v, 1, 1),
            v,
        )

    def weigh(weights, parts):
        total = weights[0] * parts[0]
        for weight, part in zip(weights[1:], parts[1:]):
            total = total + weight * part
        return total

    def operator(d, e):
        return weigh((kx[e], kx[e - 1], ky[0, e], ky[1, e], kz[0, e], kz[1, e], kb[e]), d)

    def put_weights(x):
        k = kp[x + HALO]
        p = pe[x + 1]
        upper = jnp.where(jnp.logical_and(last, x == LX - 1), 1.0, 0.5)
        lower = jnp.where(jnp.logical_and(first, x == 0), 1.0, 0.5)
        wf[0, x] = (upper * k) * (p - pe[x + 2])
        wf[1, x] = (lower * k) * (p - pe[x])
        wf[2, x] = (inner_y * k) * (p - pltpu.roll(p, NG - 1, 0))
        wf[3, x] = (inner_ym * k) * (p - pltpu.roll(p, 1, 0))
        wf[4, x] = (inner_z * k) * (p - pltpu.roll(p, NG - 1, 1))
        wf[5, x] = (inner_zm * k) * (p - pltpu.roll(p, 1, 1))
        wf[6, x] = kb[x + HALO] * p

    lhs_p = jnp.concatenate(
        [jnp.concatenate([byt[0], byt[0]], axis=1), jnp.concatenate([byt[1], byt[1]], axis=1)], axis=0
    )

    def put_proj(f, layers, ds):
        parts = []
        for x, d in zip(layers, ds):
            grad = weigh(tuple(wf[j, x] for j in range(7)), d)
            parts.append(jnp.concatenate(pieces(grad, 2), axis=0))
        got = mm(lhs_p, jnp.concatenate(parts, axis=1))
        got = got[:M] + got[M:]
        for j, x in enumerate(layers):
            pbuf[f, x] = got[:, j * NG : (j + 1) * NG]

    def put_u0(x, d):
        g = s * LX + x
        safe = jnp.clip(g, 0, NX - 1)
        load = []
        for b in range(8):
            _, cell = sensor_of(safe, b)
            load.append(jnp.where(flat == cell, rsum[x + 2, b : b + 1, :], 0.0))
        u0[x + 2] = jnp.concatenate(load, axis=0) - operator(d, x + HALO)

    def put_u1(x, d):
        u1[x + 1] = operator(d, x + HALO) * tau

    def step_x(layers, project):
        ds = [differences(xe, x + 3) for x in layers]
        for x, d in zip(layers, ds):
            put_u0(x, d)
        if project:
            put_proj(0, layers, ds)

    def step_u0(layers, project):
        ds = [differences(u0, x + 2) for x in layers]
        for x, d in zip(layers, ds):
            put_u1(x, d)
        if project:
            put_proj(1, layers, ds)

    def step_u1(layers, sums):
        ds = [differences(u1, x + 1) for x in layers]
        m0, m1, m2, m3 = sums
        for x, d in zip(layers, ds):
            second, image = d[6], operator(d, x + HALO)
            start = u0[x + 2]
            m0 = m0 + fold(start * start)
            m1 = m1 + fold(start * second)
            m2 = m2 + fold(second * second)
            m3 = m3 + fold(second * image)
        put_proj(2, layers, ds)
        return m0, m1, m2, m3

    def mix_x(layers, fresh):
        def some(j, carry):
            for f in range(3):
                kept = [pbuf[f, x] for x in layers]
                for i in (4 * j, 4 * j + 1, 4 * j + 2, 4 * j + 3):
                    total = None if fresh else qbuf[f, i]
                    for x, part in zip(layers, kept):
                        term = bx_ref[i, s * LX + x] * part
                        total = term if total is None else total + term
                    qbuf[f, i] = total
            return carry

        lax.fori_loop(0, M // 4, some, 0)

    def pairs(lo, hi, step, wide=2):
        def body(j, carry):
            step(tuple(lo + wide * j + i for i in range(wide)))
            return carry

        lax.fori_loop(0, (hi - lo) // wide, body, 0)

    def around(j):
        return j, LX - 1 - j

    load_x.wait()
    pairs(1, LX - 1, lambda layers: [put_weights(x) for x in layers])
    pairs(1, LX - 1, lambda layers: step_x(layers, True))
    pairs(2, LX - 2, lambda layers: step_u0(layers, True), 4)
    zero = jnp.zeros((8, NG), F32)
    sums = lax.fori_loop(
        0, LX // 2 - 3, lambda j, c: step_u1((3 + 2 * j, 4 + 2 * j), c), (zero, zero, zero, zero)
    )
    mix_x(range(3, 13), True)

    load_c.wait()
    pltpu.make_async_copy(cs.at[pl.ds(1, NP - 1)], cs.at[pl.ds(1, NP - 1)], c_recv).wait()
    every = cs[...]
    mine = cs[0]
    gap = every - mine[None]
    near = jnp.sum(jnp.sum(gap * gap, axis=1), axis=1, keepdims=True)
    center = jnp.sum(every, axis=0) * (1.0 / NP)
    off = every - center[None]
    spread = jnp.sum(jnp.sum(off * off, axis=0), keepdims=True) * (2.0 / (NP - 1))
    lane32 = lax.broadcasted_iota(jnp.int32, (NP, NG), 1)
    diag = lane32 == lax.broadcasted_iota(jnp.int32, (NP, NG), 0)
    near_row = jnp.sum(jnp.where(diag, near, 0.0), axis=0, keepdims=True)
    near_row = jnp.where(lane32[0:1] == NP, spread, near_row)
    tail = jnp.concatenate([jnp.broadcast_to(tau, (1, NG)), near_row, jnp.zeros((6, NG), F32)], axis=0)

    @pl.when(jnp.logical_not(first))
    def _():
        x_up().wait_recv()
        r_up().wait_recv()

    @pl.when(jnp.logical_not(last))
    def _():
        x_down().wait_recv()
        r_down().wait_recv()

    @pl.when(jnp.logical_not(first))
    def _():
        p_up().wait_recv()

    @pl.when(jnp.logical_not(last))
    def _():
        p_down().wait_recv()

    for x in around(0):
        put_weights(x)
    step_x(around(-2), False)
    step_x(around(-1), False)
    step_x(around(0), True)

    @pl.when(first)
    def _():
        u0[0:2] = jnp.zeros((2, NG, NG), F32)

    @pl.when(last)
    def _():
        u0[LX + 2 :] = jnp.zeros((2, NG, NG), F32)

    step_u0(around(-1), False)
    step_u0(around(0) + around(1), True)

    @pl.when(first)
    def _():
        u1[0:1] = jnp.zeros((1, NG, NG), F32)

    @pl.when(last)
    def _():
        u1[LX + 1 :] = jnp.zeros((1, NG, NG), F32)

    sums = step_u1(around(0) + around(1) + around(2), sums)
    mix_x((0, 1, 2, 13, 14, 15), False)

    q_two = jnp.concatenate(pieces(qbuf[...].reshape(3 * M * M, NG), 2), axis=1)
    lhs_z = jnp.concatenate(
        [jnp.concatenate([bzt[0], bzt[0]], axis=1), jnp.concatenate([bzt[1], bzt[1]], axis=1)], axis=0
    )
    tensor = mm_nt(lhs_z, q_two)
    tensor = tensor[:M] + tensor[M:]
    parts = []
    for f in range(3):
        parts += pieces(tensor[:, f * M * M : (f + 1) * M * M], 2)
    rhs = jnp.concatenate(parts, axis=0)

    m3 = sums[3] * tau
    rows = [
        jnp.broadcast_to(jnp.sum(jnp.sum(m, axis=0, keepdims=True), axis=1, keepdims=True), (1, NG))
        for m in (sums[0], sums[1], sums[2], m3)
    ]
    head = jnp.concatenate(rows, axis=0)

    for share in range(NS):
        cols = slice(share * SH, (share + 1) * SH)
        got = mm(rhs, hot[:, cols])
        low = lhot[:, cols]
        for f in range(3):
            at = 2 * M * f
            row = jnp.sum((got[at : at + M] + got[at + M : at + 2 * M]) * low, axis=0, keepdims=True)
            for q in range(SH // NG):
                pk[share, 4 * f + q : 4 * f + q + 1, :] = row[:, q * NG : (q + 1) * NG]
        pk[share, 12:16, :] = head
        pk[share, 16:24, :] = tail

        @pl.when(s != share)
        def _():
            to = rp.at[lax.rem(s - share + NS, NS)]
            remote(pk.at[share], to, r_send, r_recv, {"space": share}).start()


    rp[0] = pk[s]
    pltpu.make_async_copy(rp.at[pl.ds(1, NS - 1)], rp.at[pl.ds(1, NS - 1)], r_recv).wait()

    taus = rp[:, 16:17, :]
    least = jnp.min(taus, axis=0)
    ratio = least[None] / taus
    q0 = jnp.sum(rp[:, 12:13, :], axis=0)
    q1 = jnp.sum(rp[:, 13:14, :] * ratio, axis=0)
    q2 = jnp.sum(rp[:, 14:15, :] * (ratio * ratio), axis=0)
    q3 = jnp.sum(rp[:, 15:16, :] * (ratio * ratio * ratio), axis=0)
    proj0 = jnp.sum(rp[:, 0:4, :], axis=0)
    proj1 = jnp.sum(rp[:, 4:8, :], axis=0)
    proj2 = jnp.sum(rp[:, 8:12, :] * ratio, axis=0)
    alpha = q0 / q1
    norm = alpha * alpha * q2 - q0
    grown = norm / q0 + 1.0
    alpha1 = norm / (alpha * alpha * (q3 - q2 * (q2 / q1)))
    tau0 = least
    scale0 = tau0 * (alpha + alpha1 * grown)
    scale2 = -(tau0 * alpha1) * alpha
    gs[0] = proj0 + scale0 * proj1 + scale2 * proj2

    for j in range(NP - 1):
        r = far(j, NP)
        remote(gs.at[0], gs.at[NP - r], g_send, g_recv, peer_p(r)).start()

    scale1 = scale2 * (tau0 / tau)

    def put_x(x, carry):
        adj_ref[x] = xe[x + 3] + scale0 * u0[x + 2] + scale1 * u1[x + 1]
        return carry

    lax.fori_loop(0, LX, put_x, 0)

    near_all = jnp.sum(rp[:, 17:18, :], axis=0)
    width = near_all[:, NP : NP + 1]
    kern = jnp.exp(-near_all / width)
    kcol = jnp.sum(jnp.where(diag, kern, 0.0), axis=1, keepdims=True)
    weight = jnp.broadcast_to(kcol[:, :, None], (NP, 1, NG))
    drive = jnp.sum(weight * every, axis=0)
    repel = jnp.sum(weight * (mine[None] - every), axis=0)
    base = mine + (STEP / NP) * ((2.0 / width) * repel - drive)

    pltpu.make_async_copy(gs.at[pl.ds(1, NP - 1)], gs.at[pl.ds(1, NP - 1)], g_recv).wait()
    new_ref[...] = base - (STEP / NP) * jnp.sum(weight * gs[...], axis=0)

    def sent(ref, sem):
        pltpu.make_async_copy(ref, ref, sem).wait()

    sent(cs.at[pl.ds(1, NP - 1)], c_send)
    sent(rp.at[pl.ds(1, NS - 1)], r_send)
    sent(gs.at[pl.ds(1, NP - 1)], g_send)

    @pl.when(jnp.logical_not(last))
    def _():
        x_up().wait_send()
        p_up().wait_send()
        r_up().wait_send()

    @pl.when(jnp.logical_not(first))
    def _():
        x_down().wait_send()
        p_down().wait_send()
        r_down().wait_send()


def shards(coeffs, modes, basis_x, basis_y, basis_z, pressure, initial_adjoint, sensors, observed, precision):
    vmem = pl.BlockSpec(memory_space=pltpu.VMEM)
    hbm = pl.BlockSpec(memory_space=pltpu.HBM)
    dma = pltpu.SemaphoreType.DMA
    layers = lambda count: pltpu.VMEM((count, NG, NG), F32)
    new, adjoint = pl.pallas_call(
        kernel,
        out_shape=(
            pltpu.VMEM((SH // NG, NG), F32),
            pltpu.VMEM((LX, NG, NG), F32),
        ),
        in_specs=[hbm] * 10,
        out_specs=(vmem, vmem),
        scratch_shapes=[
            pltpu.VMEM((K // NG, NG), jnp.int32),
            pltpu.SMEM((M, NX), F32),
            pltpu.VMEM((M, NG), F32),
            pltpu.VMEM((M, NG), F32),
            pltpu.SMEM(sensors.shape, jnp.int32),
            pltpu.SMEM(sensors.shape, F32),
            pltpu.SMEM(sensors.shape, F32),
            layers(LX + 6),
            layers(LX + 2),
            layers(LX + 6),
            layers(LX + 6),
            pltpu.VMEM((2, LX + 6, NG, NG), F32),
            pltpu.VMEM((2, LX + 6, NG, NG), F32),
            layers(LX + 6),
            pltpu.VMEM((7, LX, NG, NG), F32),
            layers(LX + 4),
            layers(LX + 2),
            pltpu.VMEM((LX + 4, 8, NG), F32),
            pltpu.VMEM((M * M, K), BF16),
            pltpu.VMEM((M, K), F32),
            pltpu.VMEM((3 * M, K), BF16),
            pltpu.VMEM((M, M, NG), F32),
            pltpu.VMEM((3, LX, M, NG), F32),
            pltpu.VMEM((3, M, M, NG), F32),
            pltpu.VMEM((NP, SH // NG, NG), F32),
            pltpu.VMEM((NS, SH // NG, NG), F32),
            pltpu.VMEM((NS, 24, NG), F32),
            pltpu.VMEM((NS, 24, NG), F32),
            pltpu.VMEM((NP, SH // NG, NG), F32),
            dma((3,)), dma((7,)), dma((6,)), dma((6,)),
            dma, dma, dma, dma, dma, dma, dma,
        ],
        compiler_params=pltpu.CompilerParams(
            collective_id=0, has_side_effects=True, vmem_limit_bytes=60 * 2**20
        ),
    )(
        coeffs.reshape(NS, SH // NG, NG),
        modes.reshape(K // NG, NG),
        basis_x.T,
        basis_y.T,
        basis_z.T,
        pressure[0],
        initial_adjoint[0],
        sensors,
        observed,
        precision,
    )
    return new.reshape(1, SH), adjoint[None]


def solution(mesh):
    in_specs = (
        P("particle", None),
        P(),
        P(),
        P(),
        P(),
        P("particle", "space", None, None),
        P("particle", "space", None, None),
        P(),
        P(),
        P(),
    )
    out_specs = (P("particle", "space"), P("particle", "space", None, None))
    return jax.shard_map(shards, mesh=mesh, in_specs=in_specs, out_specs=out_specs, check_vma=False)
```
